32 devices in a mesh: rot: 4 (over y, core), tile: 8 (over z, x).
Axes of the slice: x: 2, y: 2, z: 4, core: 2. Of those that a mesh axis runs over, the one named last changes fastest.
Arguments:
- volume: float32 [8, 32, 32, 128], P('tile')
- templates: bfloat16 [32, 64000], replicated
- rot_ids: int32 [4], P('rot'), may hold values from 0 to 31
Outputs:
- soft_map: float32 [8, 32, 32, 128], P('tile', 'rot')
The draws below stay inside these ranges and needn't reach their ends.
All inputs are finite; a program needn't handle non-finite values.
Results may differ from the reference program's by a relative error of at most 0.0003.
Values sent between devices are 32-bit elements; how exact they have to be, the bound alone decides.
A program may use at most 128 MiB of HBM per device.

```python
import jax
import jax.numpy as jnp

TMPL = 40
TABLE = 32
TX = 32
TY = 32
NZ = 128
ROTS = 4
TILES = 8
GRID_Y = 8
GRID_X = 1
NXG = 32
NYG = 256


def envelope_grid():
    offsets = jnp.arange(TMPL, dtype=jnp.float32) - (TMPL - 1) / 2.0
    radius_sq = offsets[:, None, None] ** 2 + offsets[None, :, None] ** 2 + offsets[None, None, :] ** 2
    return jnp.exp(-radius_sq / (2.0 * (0.3 * TMPL) ** 2))


def draw_templates(key, part):
    key = jax.random.fold_in(key, 3)
    grids = jax.random.normal(key, (TABLE, TMPL, TMPL, TMPL), dtype=jnp.float32) * envelope_grid()[None]
    return grids.reshape(TABLE, TMPL ** 3).astype(jnp.bfloat16)


def draw_volume(key, part):
    key = jax.random.fold_in(key, 5)
    key_rows, key_cells = jax.random.split(key)
    positions = jnp.arange(NXG, dtype=jnp.float32) / max(NXG - 1, 1)
    ramp_scale = 10.0 ** (-1.7 + 2.2 * positions) * jnp.exp(jax.random.uniform(key_rows, (NXG,), minval=-0.7, maxval=0.7, dtype=jnp.float32))
    speckle = jnp.clip(jax.random.normal(key_cells, (NXG, NYG, NZ), dtype=jnp.float32), -6.0, 6.0)
    whole = speckle * ramp_scale[:, None, None]
    return whole.reshape(GRID_X, TX, GRID_Y, TY, NZ).transpose(0, 2, 1, 3, 4).reshape(TILES, TX, TY, NZ)


def with_ends(result, rng, least, largest):
    longest = result.shape.index(max(result.shape))
    spots = []
    for shift in (0, 1):
        where = [jax.random.randint(jax.random.fold_in(rng, axis), (), 0, length) for axis, length in enumerate(result.shape)]
        where[longest] = (where[longest] + shift) % result.shape[longest]
        spots.append(tuple(where))
    return result.at[spots[0]].set(least).at[spots[1]].set(largest)


def setup_inputs(seed: int = 0) -> dict:
    key_of = jax.random.split(jax.random.key(seed), 4)
    return {
        "volume": draw_volume(jax.random.fold_in(key_of[3], 71), 0),
        "templates": draw_templates(jax.random.fold_in(key_of[3], 71), 0),
        "rot_ids": with_ends(jax.random.randint(key_of[2], (ROTS,), 0, TABLE), jax.random.fold_in(key_of[2], 1), 0, TABLE - 1).astype(jnp.int32),
    }


VAR_FLOOR = 0.05
EPSILON = 1e-06
SHARPNESS = 2.0

def sphere():
    offsets = jnp.arange(TMPL, dtype=jnp.float32) - (TMPL - 1) / 2.0
    radius_sq = offsets[:, None, None] ** 2 + offsets[None, :, None] ** 2 + offsets[None, None, :] ** 2
    return (radius_sq <= (TMPL / 2.0) ** 2).astype(jnp.float32)

def normalize(flat_grid, sphere_mask, voxel_count):
    template = flat_grid.astype(jnp.float32).reshape(TMPL, TMPL, TMPL)
    centre = jnp.sum(template * sphere_mask) / voxel_count
    centred = (template - centre) * sphere_mask
    spread = jnp.sqrt(jnp.sum(centred * centred) / voxel_count + EPSILON)
    return centred / spread

def to_global(tiled):
    return tiled.reshape(GRID_X, GRID_Y, TX, TY, NZ).transpose(0, 2, 1, 3, 4).reshape(NXG, NYG, NZ)

def to_tiles(values):
    return values.reshape(GRID_X, TX, GRID_Y, TY, NZ).transpose(0, 2, 1, 3, 4).reshape(TILES, TX, TY, NZ)

def reference(volume, templates, rot_ids):
    sphere_mask = sphere()
    voxel_count = jnp.sum(sphere_mask)
    half_width = TMPL // 2
    whole_volume = to_global(volume)
    lengths = (NXG + TMPL, NYG + TMPL, NZ + TMPL)
    spectrum_v = jnp.fft.rfftn(whole_volume, s=lengths)
    spectrum_sq = jnp.fft.rfftn(whole_volume * whole_volume, s=lengths)

    def correlate(field_spec, kernel):
        kernel_spec = jnp.fft.rfftn(kernel, s=lengths)
        circular = jnp.fft.irfftn(field_spec * jnp.conj(kernel_spec), s=lengths)
        circular = jnp.roll(circular, (half_width, half_width, half_width), axis=(0, 1, 2))
        return circular[:NXG, :NYG, :NZ]
    local_mean = correlate(spectrum_v, sphere_mask) / voxel_count
    local_sq = correlate(spectrum_sq, sphere_mask) / voxel_count
    local_std = jnp.sqrt(jnp.maximum(local_sq - local_mean * local_mean, VAR_FLOOR))
    score_scale = SHARPNESS / (jnp.sqrt(voxel_count) * local_std)
    running_max = jnp.full((NXG, NYG, NZ), -jnp.inf, dtype=jnp.float32)
    running_sum = jnp.zeros((NXG, NYG, NZ), dtype=jnp.float32)
    for rotation in range(ROTS):
        kernel = normalize(templates[rot_ids[rotation]], sphere_mask, voxel_count)
        scores = correlate(spectrum_v, kernel) * score_scale
        new_max = jnp.maximum(running_max, scores)
        running_sum = running_sum * jnp.exp(running_max - new_max) + jnp.exp(scores - new_max)
        running_max = new_max
    return to_tiles(running_max + jnp.log(running_sum))
```

```python
import functools
import math

import jax
import jax.numpy as jnp
import ml_dtypes
import numpy as np
from jax import lax
from jax.experimental import pallas as pl
from jax.experimental.pallas import tpu as pltpu
from jax.sharding import PartitionSpec as P

TMPL = 40
HALF = TMPL // 2
VAR_FLOOR = 0.05
EPSILON = 1e-06
SHARPNESS = 2.0
LANES = 128
VMEM = 56 * 1024 * 1024


def sphere():
    offsets = np.arange(TMPL) - (TMPL - 1) / 2.0
    squares = offsets**2
    radius_sq = squares[:, None, None] + squares[None, :, None] + squares[None, None, :]
    return (radius_sq <= (TMPL / 2.0) ** 2).astype(np.float64)


def halves(table):
    high = table.astype(ml_dtypes.bfloat16)
    low = (table - high.astype(np.float64)).astype(ml_dtypes.bfloat16)
    return high, low


def left_table(table):
    high, low = halves(table)
    return np.concatenate([high, high, low], axis=1)


def right_table(table):
    high, low = halves(table)
    return np.concatenate([high, high, low], axis=0)


def wide(table, axis, size):
    pad = [(0, 0), (0, 0)]
    pad[axis] = (0, size - table.shape[axis])
    return np.pad(table, pad)


def angles(length, rows, columns):
    return 2.0 * math.pi * ((np.asarray(rows)[:, None] * np.asarray(columns)[None, :]) % length) / length


def y_forward(length, inputs):
    theta = angles(length, np.arange(length), np.arange(length))[:, : min(inputs, length)]
    return left_table(np.concatenate([wide(np.cos(theta), 1, inputs), wide(np.sin(theta), 1, inputs)], axis=0))


def z_forward(length, inputs, freqs):
    theta = angles(length, np.arange(inputs), np.arange(freqs))
    return right_table(np.concatenate([wide(np.cos(theta), 1, LANES), wide(np.sin(theta), 1, LANES)], axis=1))


def y_inverse(length, padded, outputs):
    theta = angles(length, np.arange(outputs), np.arange(length))
    both = np.concatenate([np.cos(theta), np.sin(theta)], axis=0) / length
    return left_table(wide(both, 1, padded))


def z_inverse(length, outputs, freqs, extra):
    theta = angles(length, np.arange(freqs), np.arange(outputs) - HALF)
    index = np.arange(freqs)
    weight = np.where((index == 0) | (2 * index == length), 1.0, 2.0)[:, None] / (length * extra)
    real = wide(np.cos(theta) * weight, 0, LANES)
    imag = wide(-np.sin(theta) * weight, 0, LANES)
    return right_table(np.concatenate([real, imag], axis=0))


def mask_spectrum(places, length_x, length_y, length_z, freqs):
    field = np.zeros((length_x, length_y, length_z))
    field[np.asarray(places), :TMPL, :TMPL] = sphere()
    spec = np.fft.rfftn(field)
    gap = ((0, 0), (0, 0), (0, LANES - freqs))
    return np.concatenate([np.pad(spec.real, gap), np.pad(spec.imag, gap)], axis=2).astype(np.float32)


def plus(a, b):
    if a is None:
        return b
    if b is None:
        return a
    return (a[0] + b[0], a[1] + b[1])


def minus(a, b):
    if b is None:
        return a
    if a is None:
        return (-b[0], -b[1])
    return (a[0] - b[0], a[1] - b[1])


def turn(a, step, length):
    if a is None:
        return None
    step %= length
    re, im = a
    eighth = 8 * step
    if eighth % length == 0:
        part = eighth // length
        root = math.sqrt(0.5)
        if part == 0:
            return a
        if part == 2:
            return (-im, re)
        if part == 4:
            return (-re, -im)
        if part == 6:
            return (im, -re)
        if part == 1:
            return ((re - im) * root, (re + im) * root)
        if part == 3:
            return ((re + im) * -root, (re - im) * root)
        if part == 5:
            return ((im - re) * root, (re + im) * -root)
        return ((re + im) * root, (im - re) * root)
    c = math.cos(2.0 * math.pi * step / length)
    s = math.sin(2.0 * math.pi * step / length)
    return (re * c - im * s, re * s + im * c)


def small_dft(values, sign):
    length = len(values)
    if length == 1:
        return values
    if length % 2 == 0:
        even = small_dft(values[0::2], sign)
        odd = small_dft(values[1::2], sign)
        odd = [turn(value, sign * k, length) for k, value in enumerate(odd)]
        return [plus(e, o) for e, o in zip(even, odd)] + [minus(e, o) for e, o in zip(even, odd)]
    sums = []
    for k in range(length):
        total = None
        for n in range(length):
            total = plus(total, turn(values[n], sign * n * k, length))
        sums.append(total)
    return sums


def pieces(values, axis):
    high = values.astype(jnp.bfloat16)
    low = (values - high.astype(jnp.float32)).astype(jnp.bfloat16)
    return jnp.concatenate([high, low, high], axis=axis)


def dot(a, b):
    return jnp.dot(a, b, preferred_element_type=jnp.float32)


def planes(pair, ly, tz, length_y):
    o = dot(ly, pieces(pair, 0))
    g = jnp.concatenate([o[:, :LANES], o[:, LANES:]], axis=0)
    h = dot(pieces(g, 1), tz)
    outs = []
    for which in range(2):
        base = 2 * length_y * which
        c = h[base : base + length_y]
        s = h[base + length_y : base + 2 * length_y]
        outs.append((c[:, :LANES] - s[:, LANES:], -s[:, :LANES] - c[:, LANES:]))
    return outs


def template_kernel(length_y, grid_ref, ly_ref, tz_ref, out_ref):
    def step(pair, carry):
        both = jnp.concatenate([grid_ref[2 * pair], grid_ref[2 * pair + 1]], axis=1)
        outs = planes(both, ly_ref[...], tz_ref[...], length_y)
        for which, (re, im) in enumerate(outs):
            out_ref[2 * pair + which, :, :LANES] = re
            out_ref[2 * pair + which, :, LANES:] = im
        return carry

    lax.fori_loop(0, TMPL // 2, step, 0, unroll=2)


def main_kernel(
    dims, places, voxels,
    ext_ref, khat_ref, mhat_hbm, phase_ref, ly_ref, tz_ref, iy_ref, iz_ref,
    score_ref, scale_ref,
    fields, mhat, stage, mixed, rows, local, sem,
):
    size_in, length_y, padded, size_x, size_y, inner, outer = dims
    length_x = inner * outer
    fetch = pltpu.make_async_copy(mhat_hbm, mhat, sem)
    fetch.start()

    def forward(x, carry):
        v = ext_ref[x]
        outs = planes(jnp.concatenate([v, v * v], axis=1), ly_ref[...], tz_ref[...], length_y)
        for which, (re, im) in enumerate(outs):
            fields[which, x, :, :LANES] = re
            fields[which, x, :, LANES:] = im
        return carry

    lax.fori_loop(0, size_in, forward, 0, unroll=2)
    rows[:, length_y:, :] = jnp.zeros((rows.shape[0], padded - length_y, 2 * LANES), jnp.float32)
    fetch.wait()

    def block(r, carry):
        at = pl.ds(pl.multiple_of(r * 8, 8), 8)

        def first(read, slot):
            for n2 in range(inner):
                values = [read(inner * n1 + n2) for n1 in range(outer)]
                for k1, value in enumerate(small_dft(values, -1)):
                    re, im = turn(value, -n2 * k1, length_x)
                    stage[slot, k1 * inner + n2, :, :LANES] = re
                    stage[slot, k1 * inner + n2, :, LANES:] = im

        def field_reader(which):
            def read(n):
                if n >= size_in:
                    return None
                return (fields[which, n, at, :LANES], fields[which, n, at, LANES:])

            return read

        def kernel_reader(n):
            if n not in places:
                return None
            q = places.index(n)
            return (khat_ref[q, at, :LANES], khat_ref[q, at, LANES:])

        first(field_reader(0), 0)
        first(field_reader(1), 1)
        first(kernel_reader, 2)

        def second(slot, k1):
            values = [
                (stage[slot, k1 * inner + n2, :, :LANES], stage[slot, k1 * inner + n2, :, LANES:])
                for n2 in range(inner)
            ]
            return small_dft(values, -1)

        def times(a, b):
            return (a[0] * b[0] + a[1] * b[1], a[1] * b[0] - a[0] * b[1])

        for k1 in range(outer):
            volume = second(0, k1)
            template = second(2, k1)
            mask = [
                (mhat[k1 + outer * k2, at, :LANES], mhat[k1 + outer * k2, at, LANES:])
                for k2 in range(inner)
            ]
            square = second(1, k1)
            products = (
                [times(a, b) for a, b in zip(volume, template)],
                [times(a, b) for a, b in zip(volume, mask)],
                [times(a, b) for a, b in zip(square, mask)],
            )
            for slot, product in enumerate(products):
                for n2, value in enumerate(small_dft(product, 1)):
                    re, im = turn(value, n2 * k1, length_x)
                    mixed[slot, k1 * inner + n2, :, :LANES] = re
                    mixed[slot, k1 * inner + n2, :, LANES:] = im

        for n2 in range(inner):
            def load(slot):
                return [
                    (mixed[slot, k1 * inner + n2, :, :LANES], mixed[slot, k1 * inner + n2, :, LANES:])
                    for k1 in range(outer)
                ]

            sums = small_dft(load(0), 1)
            for n1 in range(size_x // inner):
                rows[inner * n1 + n2, at, :LANES] = sums[n1][0]
                rows[inner * n1 + n2, at, LANES:] = sums[n1][1]
            for slot in (1, 2):
                re_sum = None
                for k1, (re, im) in enumerate(load(slot)):
                    c, s = phase_ref[k1, 0], phase_ref[k1, 1]
                    re_part, im_part = re * c - im * s, re * s + im * c
                    if re_sum is None:
                        re_sum, im_sum = re_part, im_part
                    else:
                        re_sum, im_sum = re_sum + re_part, im_sum + im_part
                target = size_x + (slot - 1) * inner + n2
                rows[target, at, :LANES] = re_sum
                rows[target, at, LANES:] = im_sum
        return carry

    lax.fori_loop(0, length_y // 8, block, 0)

    group = 4

    def inverse(step, carry):
        flat = []
        for i in range(group):
            o = dot(iy_ref[...], pieces(rows[step * group + i], 0))
            c, s = o[:size_y], o[size_y:]
            re = c[:, :LANES] - s[:, LANES:]
            im = c[:, LANES:] + s[:, :LANES]
            flat.append(jnp.concatenate([re, im], axis=1))
        result = dot(pieces(jnp.concatenate(flat, axis=0), 1), iz_ref[...])
        for i in range(group):
            local[step * group + i] = result[i * size_y : (i + 1) * size_y]
        return carry

    lax.fori_loop(0, (size_x + 2 * inner) // group, inverse, 0)
    score_ref[...] = local[:size_x]
    mean = local[size_x : size_x + inner] / voxels
    square = local[size_x + inner :] / voxels
    std = jnp.sqrt(jnp.maximum(square - mean * mean, VAR_FLOOR))
    scale_ref[...] = SHARPNESS / (math.sqrt(voxels) * std)


def normalize(flat_grid, sphere_mask, voxel_count):
    template = flat_grid.astype(jnp.float32).reshape(TMPL, TMPL, TMPL)
    centre = jnp.sum(template * sphere_mask) / voxel_count
    centred = (template - centre) * sphere_mask
    spread = jnp.sqrt(jnp.sum(centred * centred) / voxel_count + EPSILON)
    return centred / spread


def halo(block, distance, across, axis):
    tiles = lax.axis_size("tile")
    stays = lambda t: distance > 1 or t % across != 0
    up = [(t - distance, t) for t in range(distance, tiles) if distance >= across or t % across != 0]
    down = [(t, s) for s, t in up]
    size = block.shape[axis]
    lower = lax.ppermute(lax.slice_in_dim(block, size - HALF, size, axis=axis), "tile", up)
    upper = lax.ppermute(lax.slice_in_dim(block, 0, HALF, axis=axis), "tile", down)
    return lower, upper


def shards(volume, templates, rot_ids):
    tile_count = lax.axis_size("tile")
    rots = lax.axis_size("rot")
    across = min(tile_count, 8)
    down = tile_count // across
    block = volume[0]
    size_x, size_y, size_z = block.shape
    inner = size_x // rots
    if down > 1:
        lower, upper = halo(block, across, across, 0)
        block = jnp.concatenate([lower, block, upper], axis=0)
        length_x = size_x + TMPL
        places = tuple(range(TMPL))
    else:
        length_x = -(-(size_x + HALF) // (2 * inner)) * 2 * inner
        places = tuple((q - HALF) % length_x for q in range(TMPL))
    outer = length_x // inner
    size_in = block.shape[0]
    length_y = size_y + TMPL
    padded = -(-length_y // 16) * 16
    length_z = size_z + HALF
    freqs = length_z // 2 + 1

    mask = sphere()
    voxels = float(mask.sum())
    if across > 1:
        lower, upper = halo(block, 1, across, 1)
    else:
        lower = upper = jnp.zeros((size_in, HALF, size_z), jnp.float32)
    bottom = jnp.zeros((size_in, padded - length_y, size_z), jnp.float32)
    extended = jnp.concatenate([lower, block, upper, bottom], axis=1)

    tz = jnp.asarray(z_forward(length_z, LANES, freqs))
    kernel = normalize(templates[rot_ids[0]], jnp.asarray(mask, jnp.float32), voxels)
    kernel_rows = 48
    kernel = jnp.pad(kernel, ((0, 0), (0, kernel_rows - TMPL), (0, LANES - TMPL)))
    vmem = pl.BlockSpec(memory_space=pltpu.VMEM)
    khat = pl.pallas_call(
        functools.partial(template_kernel, length_y),
        out_shape=jax.ShapeDtypeStruct((TMPL, length_y, 2 * LANES), jnp.float32),
        in_specs=[vmem] * 3,
        out_specs=vmem,
        compiler_params=pltpu.CompilerParams(vmem_limit_bytes=VMEM),
        cost_estimate=pl.CostEstimate(flops=4 * 10**9, bytes_accessed=4 * 10**6, transcendentals=0),
        name="template_spectrum",
    )(kernel, jnp.asarray(y_forward(length_y, kernel_rows)), tz)

    mhat = jnp.asarray(mask_spectrum(places, length_x, length_y, length_z, freqs))
    angle = (jnp.arange(outer) * lax.axis_index("rot") % outer).astype(jnp.float32) * (2.0 * math.pi / outer)
    phase = jnp.stack([jnp.cos(angle), jnp.sin(angle)], axis=1)
    dims = (size_in, length_y, padded, size_x, size_y, inner, outer)
    scores, scale = pl.pallas_call(
        functools.partial(main_kernel, dims, places, voxels),
        out_shape=(
            jax.ShapeDtypeStruct((size_x, size_y, size_z), jnp.float32),
            jax.ShapeDtypeStruct((inner, size_y, size_z), jnp.float32),
        ),
        in_specs=[
            vmem, vmem, pl.BlockSpec(memory_space=pl.ANY), pl.BlockSpec(memory_space=pltpu.SMEM),
            vmem, vmem, vmem, vmem,
        ],
        out_specs=(vmem, vmem),
        scratch_shapes=[
            pltpu.VMEM((2, size_in, length_y, 2 * LANES), jnp.float32),
            pltpu.VMEM((length_x, length_y, 2 * LANES), jnp.float32),
            pltpu.VMEM((3, length_x, 8, 2 * LANES), jnp.float32),
            pltpu.VMEM((3, length_x, 8, 2 * LANES), jnp.float32),
            pltpu.VMEM((size_x + 2 * inner, padded, 2 * LANES), jnp.float32),
            pltpu.VMEM((size_x + 2 * inner, size_y, size_z), jnp.float32),
            pltpu.SemaphoreType.DMA,
        ],
        compiler_params=pltpu.CompilerParams(vmem_limit_bytes=VMEM),
        name="correlate",
    )(
        extended, khat, mhat, phase,
        jnp.asarray(y_forward(length_y, padded)), tz,
        jnp.asarray(y_inverse(length_y, padded, size_y)),
        jnp.asarray(z_inverse(length_z, size_z, freqs, length_x)),
    )
    gathered = lax.all_to_all(scores, "rot", split_axis=0, concat_axis=0, tiled=True)
    gathered = gathered.reshape(rots, inner, size_y, size_z) * scale[None]
    largest = jnp.max(gathered, axis=0)
    return (largest + jnp.log(jnp.sum(jnp.exp(gathered - largest[None]), axis=0)))[None]


def solution(mesh):
    return jax.shard_map(
        shards,
        mesh=mesh,
        in_specs=(P("tile", None, None, None), P(), P("rot")),
        out_specs=P("tile", "rot", None, None),
        check_vma=False,
    )
```

```python
import functools
import math

import jax
import jax.numpy as jnp
import ml_dtypes
import numpy as np
from jax import lax
from jax.experimental import pallas as pl
from jax.experimental.pallas import tpu as pltpu
from jax.sharding import PartitionSpec as P

TMPL = 40
HALF = TMPL // 2
VAR_FLOOR = 0.05
EPSILON = 1e-06
SHARPNESS = 2.0
LANES = 128
VMEM = 56 * 1024 * 1024


def sphere():
    offsets = np.arange(TMPL) - (TMPL - 1) / 2.0
    squares = offsets**2
    radius_sq = squares[:, None, None] + squares[None, :, None] + squares[None, None, :]
    return (radius_sq <= (TMPL / 2.0) ** 2).astype(np.float64)


def halves(table):
    high = table.astype(ml_dtypes.bfloat16)
    low = (table - high.astype(np.float64)).astype(ml_dtypes.bfloat16)
    return high, low


def left_table(table):
    high, low = halves(table)
    return np.concatenate([high, high, low], axis=1)


def right_table(table):
    high, low = halves(table)
    return np.concatenate([high, high, low], axis=0)


def wide(table, axis, size):
    pad = [(0, 0), (0, 0)]
    pad[axis] = (0, size - table.shape[axis])
    return np.pad(table, pad)


def angles(length, rows, columns):
    return 2.0 * math.pi * ((np.asarray(rows)[:, None] * np.asarray(columns)[None, :]) % length) / length


def y_forward(length, inputs, offset):
    y = np.arange(inputs) - offset
    theta = angles(length, np.arange(length), y)
    inside = ((y >= 0) & (y < length))[None, :]
    return left_table(np.concatenate([np.cos(theta) * inside, np.sin(theta) * inside], axis=0))


def z_forward(length, inputs, freqs):
    theta = angles(length, np.arange(inputs), np.arange(freqs))
    return right_table(np.concatenate([wide(np.cos(theta), 1, LANES), wide(np.sin(theta), 1, LANES)], axis=1))


def y_inverse(length, padded, outputs):
    theta = angles(length, np.arange(outputs), np.arange(length))
    both = np.concatenate([np.cos(theta), np.sin(theta)], axis=0) / length
    return left_table(wide(both, 1, padded))


def z_inverse(length, outputs, freqs, extra):
    theta = angles(length, np.arange(freqs), np.arange(outputs) - HALF)
    index = np.arange(freqs)
    weight = np.where((index == 0) | (2 * index == length), 1.0, 2.0)[:, None] / (length * extra)
    real = wide(np.cos(theta) * weight, 0, LANES)
    imag = wide(-np.sin(theta) * weight, 0, LANES)
    return right_table(np.concatenate([real, imag], axis=0))


def mask_spectrum(places, length_x, length_y, length_z, freqs):
    field = np.zeros((length_x, length_y, length_z))
    field[np.asarray(places), :TMPL, :TMPL] = sphere()
    spec = np.fft.rfftn(field)
    gap = ((0, 0), (0, 0), (0, LANES - freqs))
    return np.concatenate([np.pad(spec.real, gap), np.pad(spec.imag, gap)], axis=2).astype(np.float32)


def plus(a, b):
    if a is None:
        return b
    if b is None:
        return a
    return (a[0] + b[0], a[1] + b[1])


def minus(a, b):
    if b is None:
        return a
    if a is None:
        return (-b[0], -b[1])
    return (a[0] - b[0], a[1] - b[1])


def turn(a, step, length):
    if a is None:
        return None
    step %= length
    re, im = a
    eighth = 8 * step
    if eighth % length == 0:
        part = eighth // length
        root = math.sqrt(0.5)
        if part == 0:
            return a
        if part == 2:
            return (-im, re)
        if part == 4:
            return (-re, -im)
        if part == 6:
            return (im, -re)
        if part == 1:
            return ((re - im) * root, (re + im) * root)
        if part == 3:
            return ((re + im) * -root, (re - im) * root)
        if part == 5:
            return ((im - re) * root, (re + im) * -root)
        return ((re + im) * root, (im - re) * root)
    c = math.cos(2.0 * math.pi * step / length)
    s = math.sin(2.0 * math.pi * step / length)
    return (re * c - im * s, re * s + im * c)


def small_dft(values, sign):
    length = len(values)
    if length == 1:
        return values
    if length % 2 == 0:
        even = small_dft(values[0::2], sign)
        odd = small_dft(values[1::2], sign)
        odd = [turn(value, sign * k, length) for k, value in enumerate(odd)]
        return [plus(e, o) for e, o in zip(even, odd)] + [minus(e, o) for e, o in zip(even, odd)]
    sums = []
    for k in range(length):
        total = None
        for n in range(length):
            total = plus(total, turn(values[n], sign * n * k, length))
        sums.append(total)
    return sums


def pieces(values, axis):
    high = values.astype(jnp.bfloat16)
    low = (values - high.astype(jnp.float32)).astype(jnp.bfloat16)
    return jnp.concatenate([high, low, high], axis=axis)


def dot(a, b):
    return jnp.dot(a, b, preferred_element_type=jnp.float32)


def planes(pairs, ly, tz, length_y):
    flat = []
    for pair in pairs:
        o = dot(ly, pieces(pair, 0))
        flat += [o[:, :LANES], o[:, LANES:]]
    h = dot(pieces(jnp.concatenate(flat, axis=0), 1), tz)
    outs = []
    for which in range(2 * len(pairs)):
        base = 2 * length_y * which
        c = h[base : base + length_y]
        s = h[base + length_y : base + 2 * length_y]
        outs.append((c[:, :LANES] - s[:, LANES:], -s[:, :LANES] - c[:, LANES:]))
    return outs


def template_kernel(
    length_y, across, rim, voxels, grid_ref, block_ref, ly_ref, tz_ref, out_ref, ext_ref, send_sem, recv_sem
):
    tile = lax.axis_index("tile")
    column = lax.rem(tile, across)
    before, after = column > 0, column < across - 1
    size_y = block_ref.shape[1]
    barrier = pltpu.get_barrier_semaphore()

    def to_next():
        return pltpu.make_async_remote_copy(
            src_ref=block_ref.at[:, pl.ds(size_y - rim, rim), :],
            dst_ref=ext_ref.at[:, pl.ds(0, rim), :],
            send_sem=send_sem.at[0],
            recv_sem=recv_sem.at[0],
            device_id={"tile": tile + 1},
            device_id_type=pl.DeviceIdType.MESH,
        )

    def to_previous():
        return pltpu.make_async_remote_copy(
            src_ref=block_ref.at[:, pl.ds(0, rim), :],
            dst_ref=ext_ref.at[:, pl.ds(rim + size_y, rim), :],
            send_sem=send_sem.at[1],
            recv_sem=recv_sem.at[1],
            device_id={"tile": tile - 1},
            device_id_type=pl.DeviceIdType.MESH,
        )

    @pl.when(before)
    def _():
        pl.semaphore_signal(barrier, inc=1, device_id={"tile": tile - 1}, device_id_type=pl.DeviceIdType.MESH)

    @pl.when(after)
    def _():
        pl.semaphore_signal(barrier, inc=1, device_id={"tile": tile + 1}, device_id_type=pl.DeviceIdType.MESH)

    shape = grid_ref.shape[1:]
    odd_y = 2 * lax.broadcasted_iota(jnp.int32, shape, 0) - (TMPL - 1)
    odd_z = 2 * lax.broadcasted_iota(jnp.int32, shape, 1) - (TMPL - 1)
    plane_sq = odd_y * odd_y + odd_z * odd_z

    def masked(q, centre):
        odd_x = 2 * q - (TMPL - 1)
        inside = plane_sq + odd_x * odd_x <= TMPL * TMPL
        return jnp.where(inside, grid_ref[q].astype(jnp.float32) - centre, 0.0)

    zeros = jnp.zeros(shape, jnp.float32)
    total = lax.fori_loop(0, TMPL, lambda q, held: held + masked(q, 0.0), zeros, unroll=4)
    centre = jnp.sum(total) / voxels

    def add_square(q, held):
        value = masked(q, centre)
        return held + value * value

    squares = jnp.sum(lax.fori_loop(0, TMPL, add_square, zeros, unroll=4), keepdims=True)
    scale = 1.0 / jnp.sqrt(squares / voxels + EPSILON)

    pl.semaphore_wait(barrier, before.astype(jnp.int32) + after.astype(jnp.int32))

    @pl.when(before)
    def _():
        to_previous().start()

    @pl.when(after)
    def _():
        to_next().start()

    ext_ref[:, rim : rim + size_y, :] = block_ref[...]
    nothing = jnp.zeros((block_ref.shape[0], rim, LANES), jnp.float32)

    @pl.when(jnp.logical_not(before))
    def _():
        ext_ref[:, :rim, :] = nothing

    @pl.when(jnp.logical_not(after))
    def _():
        ext_ref[:, rim + size_y :, :] = nothing

    group = 4

    def step(index, carry):
        pairs = []
        for i in range(group):
            q = 2 * (index * group + i)
            pairs.append(jnp.concatenate([masked(q, centre) * scale, masked(q + 1, centre) * scale], axis=1))
        for which, (re, im) in enumerate(planes(pairs, ly_ref[...], tz_ref[...], length_y)):
            out_ref[2 * group * index + which, :, :LANES] = re
            out_ref[2 * group * index + which, :, LANES:] = im
        return carry

    lax.fori_loop(0, TMPL // (2 * group), step, 0)

    @pl.when(before)
    def _():
        to_previous().wait_send()
        to_next().wait_recv()

    @pl.when(after)
    def _():
        to_next().wait_send()
        to_previous().wait_recv()


def exchange_kernel(rots, score_ref, scale_ref, out_ref, others, send_sem, recv_sem):
    me = lax.axis_index("rot")
    rows = scale_ref.shape[0]
    barrier = pltpu.get_barrier_semaphore()
    peers = [lax.rem(me + d, rots) for d in range(1, rots)]
    for peer in peers:
        pl.semaphore_signal(barrier, inc=1, device_id={"rot": peer}, device_id_type=pl.DeviceIdType.MESH)
    pl.semaphore_wait(barrier, rots - 1)
    copies = []
    for d, peer in enumerate(peers):
        copy = pltpu.make_async_remote_copy(
            src_ref=score_ref.at[pl.ds(peer * rows, rows)],
            dst_ref=others.at[d],
            send_sem=send_sem.at[d],
            recv_sem=recv_sem.at[d],
            device_id={"rot": peer},
            device_id_type=pl.DeviceIdType.MESH,
        )
        copy.start()
        copies.append(copy)
    scale = scale_ref[...]
    scores = [score_ref[pl.ds(me * rows, rows)] * scale]
    for copy in copies:
        copy.wait()
    for d in range(rots - 1):
        scores.append(others[d] * scale)
    largest = functools.reduce(jnp.maximum, scores)
    total = functools.reduce(jnp.add, [jnp.exp(score - largest) for score in scores])
    out_ref[...] = largest + jnp.log(total)


def main_kernel(
    dims, places, voxels,
    ext_ref, khat_ref, mhat_hbm, phase_ref, ly_ref, tz_ref, iy_ref, iz_ref,
    score_ref, scale_ref,
    fields, mhat, stage, mixed, rows, local, sem,
):
    size_in, length_y, padded, size_x, size_y, inner, outer = dims
    length_x = inner * outer
    fetch = pltpu.make_async_copy(mhat_hbm, mhat, sem)
    fetch.start()

    def forward(step, carry):
        pairs = []
        for i in range(4):
            v = ext_ref[4 * step + i]
            pairs.append(jnp.concatenate([v, v * v], axis=1))
        for which, (re, im) in enumerate(planes(pairs, ly_ref[...], tz_ref[...], length_y)):
            fields[which % 2, 4 * step + which // 2, :, :LANES] = re
            fields[which % 2, 4 * step + which // 2, :, LANES:] = im
        return carry

    lax.fori_loop(0, size_in // 4, forward, 0)
    rows[:, length_y:, :] = jnp.zeros((rows.shape[0], padded - length_y, 2 * LANES), jnp.float32)
    fetch.wait()

    def block(r, carry):
        at = pl.ds(pl.multiple_of(r * 8, 8), 8)

        def first(read, slot):
            for n2 in range(inner):
                values = [read(inner * n1 + n2) for n1 in range(outer)]
                for k1, value in enumerate(small_dft(values, -1)):
                    re, im = turn(value, -n2 * k1, length_x)
                    stage[slot, k1 * inner + n2, :, :LANES] = re
                    stage[slot, k1 * inner + n2, :, LANES:] = im

        def field_reader(which):
            def read(n):
                if n >= size_in:
                    return None
                return (fields[which, n, at, :LANES], fields[which, n, at, LANES:])

            return read

        def kernel_reader(n):
            if n not in places:
                return None
            q = places.index(n)
            return (khat_ref[q, at, :LANES], khat_ref[q, at, LANES:])

        first(field_reader(0), 0)
        first(field_reader(1), 1)
        first(kernel_reader, 2)

        def second(slot, k1):
            values = [
                (stage[slot, k1 * inner + n2, :, :LANES], stage[slot, k1 * inner + n2, :, LANES:])
                for n2 in range(inner)
            ]
            return small_dft(values, -1)

        def times(a, b):
            return (a[0] * b[0] + a[1] * b[1], a[1] * b[0] - a[0] * b[1])

        for k1 in range(outer):
            volume = second(0, k1)
            template = second(2, k1)
            mask = [
                (mhat[k1 + outer * k2, at, :LANES], mhat[k1 + outer * k2, at, LANES:])
                for k2 in range(inner)
            ]
            square = second(1, k1)
            products = (
                [times(a, b) for a, b in zip(volume, template)],
                [times(a, b) for a, b in zip(volume, mask)],
                [times(a, b) for a, b in zip(square, mask)],
            )
            for slot, product in enumerate(products):
                for n2, value in enumerate(small_dft(product, 1)):
                    re, im = turn(value, n2 * k1, length_x)
                    mixed[slot, k1 * inner + n2, :, :LANES] = re
                    mixed[slot, k1 * inner + n2, :, LANES:] = im

        for n2 in range(inner):
            def load(slot):
                return [
                    (mixed[slot, k1 * inner + n2, :, :LANES], mixed[slot, k1 * inner + n2, :, LANES:])
                    for k1 in range(outer)
                ]

            sums = small_dft(load(0), 1)
            for n1 in range(size_x // inner):
                rows[inner * n1 + n2, at, :LANES] = sums[n1][0]
                rows[inner * n1 + n2, at, LANES:] = sums[n1][1]
            for slot in (1, 2):
                re_sum = None
                for k1, (re, im) in enumerate(load(slot)):
                    c, s = phase_ref[k1, 0], phase_ref[k1, 1]
                    re_part, im_part = re * c - im * s, re * s + im * c
                    if re_sum is None:
                        re_sum, im_sum = re_part, im_part
                    else:
                        re_sum, im_sum = re_sum + re_part, im_sum + im_part
                target = size_x + (slot - 1) * inner + n2
                rows[target, at, :LANES] = re_sum
                rows[target, at, LANES:] = im_sum
        return carry

    lax.fori_loop(0, length_y // 8, block, 0)

    group = 8

    def inverse(step, carry):
        flat = []
        for i in range(group):
            o = dot(iy_ref[...], pieces(rows[step * group + i], 0))
            c, s = o[:size_y], o[size_y:]
            re = c[:, :LANES] - s[:, LANES:]
            im = c[:, LANES:] + s[:, :LANES]
            flat.append(jnp.concatenate([re, im], axis=1))
        result = dot(pieces(jnp.concatenate(flat, axis=0), 1), iz_ref[...])
        for i in range(group):
            local[step * group + i] = result[i * size_y : (i + 1) * size_y]
        return carry

    lax.fori_loop(0, (size_x + 2 * inner) // group, inverse, 0)
    score_ref[...] = local[:size_x]
    mean = local[size_x : size_x + inner] / voxels
    square = local[size_x + inner :] / voxels
    std = jnp.sqrt(jnp.maximum(square - mean * mean, VAR_FLOOR))
    scale_ref[...] = SHARPNESS / (math.sqrt(voxels) * std)


def row_halo(block, across):
    tiles = lax.axis_size("tile")
    up = [(t - across, t) for t in range(across, tiles)]
    down = [(t, s) for s, t in up]
    lower = lax.ppermute(block[block.shape[0] - HALF :], "tile", up)
    upper = lax.ppermute(block[:HALF], "tile", down)
    return jnp.concatenate([lower, block, upper], axis=0)


def shards(volume, templates, rot_ids):
    tile_count = lax.axis_size("tile")
    rots = lax.axis_size("rot")
    across = min(tile_count, 8)
    down = tile_count // across
    block = volume[0]
    size_x, size_y, size_z = block.shape
    inner = size_x // rots
    if down > 1:
        block = row_halo(block, across)
        length_x = size_x + TMPL
        places = tuple(range(TMPL))
    else:
        length_x = -(-(size_x + HALF) // (2 * inner)) * 2 * inner
        places = tuple((q - HALF) % length_x for q in range(TMPL))
    outer = length_x // inner
    size_in = block.shape[0]
    length_y = size_y + TMPL
    padded = -(-length_y // 16) * 16
    length_z = size_z + HALF
    freqs = length_z // 2 + 1

    mask = sphere()
    voxels = float(mask.sum())
    rim = -(-HALF // 8) * 8
    reach = size_y + 2 * rim
    tz = jnp.asarray(z_forward(length_z, LANES, freqs))
    kernel_rows = 48
    grid = templates[rot_ids[0]].reshape(TMPL, TMPL, TMPL)
    grid = jnp.pad(grid, ((0, 0), (0, kernel_rows - TMPL), (0, LANES - TMPL)))
    vmem = pl.BlockSpec(memory_space=pltpu.VMEM)
    khat, extended = pl.pallas_call(
        functools.partial(template_kernel, length_y, across, rim, voxels),
        out_shape=(
            jax.ShapeDtypeStruct((TMPL, length_y, 2 * LANES), jnp.float32),
            jax.ShapeDtypeStruct((size_in, reach, size_z), jnp.float32),
        ),
        in_specs=[vmem] * 4,
        out_specs=(vmem, vmem),
        scratch_shapes=[pltpu.SemaphoreType.DMA((2,)), pltpu.SemaphoreType.DMA((2,))],
        compiler_params=pltpu.CompilerParams(vmem_limit_bytes=VMEM, collective_id=0, has_side_effects=True),
        name="template_spectrum",
    )(grid, block, jnp.asarray(y_forward(length_y, kernel_rows, 0)), tz)

    mhat = jnp.asarray(mask_spectrum(places, length_x, length_y, length_z, freqs))
    angle = (jnp.arange(outer) * lax.axis_index("rot") % outer).astype(jnp.float32) * (2.0 * math.pi / outer)
    phase = jnp.stack([jnp.cos(angle), jnp.sin(angle)], axis=1)
    dims = (size_in, length_y, padded, size_x, size_y, inner, outer)
    scores, scale = pl.pallas_call(
        functools.partial(main_kernel, dims, places, voxels),
        out_shape=(
            jax.ShapeDtypeStruct((size_x, size_y, size_z), jnp.float32),
            jax.ShapeDtypeStruct((inner, size_y, size_z), jnp.float32),
        ),
        in_specs=[
            vmem, vmem, pl.BlockSpec(memory_space=pl.ANY), pl.BlockSpec(memory_space=pltpu.SMEM),
            vmem, vmem, vmem, vmem,
        ],
        out_specs=(vmem, vmem),
        scratch_shapes=[
            pltpu.VMEM((2, size_in, length_y, 2 * LANES), jnp.float32),
            pltpu.VMEM((length_x, length_y, 2 * LANES), jnp.float32),
            pltpu.VMEM((3, length_x, 8, 2 * LANES), jnp.float32),
            pltpu.VMEM((3, length_x, 8, 2 * LANES), jnp.float32),
            pltpu.VMEM((size_x + 2 * inner, padded, 2 * LANES), jnp.float32),
            pltpu.VMEM((size_x + 2 * inner, size_y, size_z), jnp.float32),
            pltpu.SemaphoreType.DMA,
        ],
        compiler_params=pltpu.CompilerParams(vmem_limit_bytes=VMEM),
        name="correlate",
    )(
        extended, khat, mhat, phase,
        jnp.asarray(y_forward(length_y, reach, rim - HALF)), tz,
        jnp.asarray(y_inverse(length_y, padded, size_y)),
        jnp.asarray(z_inverse(length_z, size_z, freqs, length_x)),
    )
    result = pl.pallas_call(
        functools.partial(exchange_kernel, rots),
        out_shape=jax.ShapeDtypeStruct((inner, size_y, size_z), jnp.float32),
        in_specs=[vmem, vmem],
        out_specs=vmem,
        scratch_shapes=[
            pltpu.VMEM((rots - 1, inner, size_y, size_z), jnp.float32),
            pltpu.SemaphoreType.DMA((rots - 1,)),
            pltpu.SemaphoreType.DMA((rots - 1,)),
        ],
        compiler_params=pltpu.CompilerParams(vmem_limit_bytes=VMEM, collective_id=1, has_side_effects=True),
        name="exchange",
    )(scores, scale)
    return result[None]


def solution(mesh):
    return jax.shard_map(
        shards,
        mesh=mesh,
        in_specs=(P("tile", None, None, None), P(), P("rot")),
        out_specs=P("tile", "rot", None, None),
        check_vma=False,
    )
```

```python
import functools
import math

import jax
import jax.numpy as jnp
import ml_dtypes
import numpy as np
from jax import lax
from jax.experimental import pallas as pl
from jax.experimental.pallas import tpu as pltpu
from jax.sharding import PartitionSpec as P

TMPL = 40
HALF = TMPL // 2
VAR_FLOOR = 0.05
EPSILON = 1e-06
SHARPNESS = 2.0
LANES = 128
VMEM = 56 * 1024 * 1024


def sphere():
    offsets = np.arange(TMPL) - (TMPL - 1) / 2.0
    squares = offsets**2
    radius_sq = squares[:, None, None] + squares[None, :, None] + squares[None, None, :]
    return (radius_sq <= (TMPL / 2.0) ** 2).astype(np.float64)


def halves(table):
    high = table.astype(ml_dtypes.bfloat16)
    low = (table - high.astype(np.float64)).astype(ml_dtypes.bfloat16)
    return high, low


def left_table(table):
    high, low = halves(table)
    return np.concatenate([high, high, low], axis=1)


def right_table(table):
    high, low = halves(table)
    return np.concatenate([high, high, low], axis=0)


def wide(table, axis, size):
    pad = [(0, 0), (0, 0)]
    pad[axis] = (0, size - table.shape[axis])
    return np.pad(table, pad)


def angles(length, rows, columns):
    return 2.0 * math.pi * ((np.asarray(rows)[:, None] * np.asarray(columns)[None, :]) % length) / length


def y_forward(length, inputs, offset):
    y = np.arange(inputs) - offset
    theta = angles(length, np.arange(length), y)
    inside = ((y >= 0) & (y < length))[None, :]
    return left_table(np.concatenate([np.cos(theta) * inside, np.sin(theta) * inside], axis=0))


def z_forward(length, inputs, freqs):
    theta = angles(length, np.arange(inputs), np.arange(freqs))
    return right_table(np.concatenate([wide(np.cos(theta), 1, LANES), wide(np.sin(theta), 1, LANES)], axis=1))


def y_inverse(length, padded, outputs):
    theta = angles(length, np.arange(outputs), np.arange(length))
    both = np.concatenate([np.cos(theta), np.sin(theta)], axis=0) / length
    return left_table(wide(both, 1, padded))


def z_inverse(length, outputs, freqs, extra):
    theta = angles(length, np.arange(freqs), np.arange(outputs) - HALF)
    index = np.arange(freqs)
    weight = np.where((index == 0) | (2 * index == length), 1.0, 2.0)[:, None] / (length * extra)
    real = wide(np.cos(theta) * weight, 0, LANES)
    imag = wide(-np.sin(theta) * weight, 0, LANES)
    return right_table(np.concatenate([real, imag], axis=0))


def mask_spectrum(places, length_x, length_y, length_z, freqs):
    field = np.zeros((length_x, length_y, length_z))
    field[np.asarray(places), :TMPL, :TMPL] = sphere()
    spec = np.fft.rfftn(field)
    gap = ((0, 0), (0, 0), (0, LANES - freqs))
    return np.concatenate([np.pad(spec.real, gap), np.pad(spec.imag, gap)], axis=2).astype(np.float32)


def plus(a, b):
    if a is None:
        return b
    if b is None:
        return a
    return (a[0] + b[0], a[1] + b[1])


def minus(a, b):
    if b is None:
        return a
    if a is None:
        return (-b[0], -b[1])
    return (a[0] - b[0], a[1] - b[1])


def turn(a, step, length):
    if a is None:
        return None
    step %= length
    re, im = a
    eighth = 8 * step
    if eighth % length == 0:
        part = eighth // length
        root = math.sqrt(0.5)
        if part == 0:
            return a
        if part == 2:
            return (-im, re)
        if part == 4:
            return (-re, -im)
        if part == 6:
            return (im, -re)
        if part == 1:
            return ((re - im) * root, (re + im) * root)
        if part == 3:
            return ((re + im) * -root, (re - im) * root)
        if part == 5:
            return ((im - re) * root, (re + im) * -root)
        return ((re + im) * root, (im - re) * root)
    c = math.cos(2.0 * math.pi * step / length)
    s = math.sin(2.0 * math.pi * step / length)
    return (re * c - im * s, re * s + im * c)


def small_dft(values, sign):
    length = len(values)
    if length == 1:
        return values
    if length % 2 == 0:
        even = small_dft(values[0::2], sign)
        odd = small_dft(values[1::2], sign)
        odd = [turn(value, sign * k, length) for k, value in enumerate(odd)]
        return [plus(e, o) for e, o in zip(even, odd)] + [minus(e, o) for e, o in zip(even, odd)]
    sums = []
    for k in range(length):
        total = None
        for n in range(length):
            total = plus(total, turn(values[n], sign * n * k, length))
        sums.append(total)
    return sums


def pieces(values, axis):
    high = values.astype(jnp.bfloat16)
    low = (values - high.astype(jnp.float32)).astype(jnp.bfloat16)
    return jnp.concatenate([high, low, high], axis=axis)


def dot(a, b):
    return jnp.dot(a, b, preferred_element_type=jnp.float32)


def planes(pairs, ly, tz, length_y):
    flat = []
    for pair in pairs:
        o = dot(ly, pieces(pair, 0))
        flat += [o[:, :LANES], o[:, LANES:]]
    h = dot(pieces(jnp.concatenate(flat, axis=0), 1), tz)
    outs = []
    for which in range(2 * len(pairs)):
        base = 2 * length_y * which
        c = h[base : base + length_y]
        s = h[base + length_y : base + 2 * length_y]
        outs.append((c[:, :LANES] - s[:, LANES:], -s[:, :LANES] - c[:, LANES:]))
    return outs


def template_kernel(
    length_y, across, rim, voxels, raw_ref, block_ref, ly_ref, tz_ref, out_ref, ext_ref,
    grid_ref, send_sem, recv_sem,
):
    tile = lax.axis_index("tile")
    core = lax.rem(lax.axis_index("rot"), 2)
    mate = lax.axis_index("rot") + 1 - 2 * core
    depth = block_ref.shape[0] // 2
    half = pl.ds(core * depth, depth)
    column = lax.rem(tile, across)
    before, after = column > 0, column < across - 1
    size_y = block_ref.shape[1]
    barrier = pltpu.get_barrier_semaphore()

    def to_next():
        return pltpu.make_async_remote_copy(
            src_ref=block_ref.at[half, pl.ds(size_y - rim, rim), :],
            dst_ref=ext_ref.at[half, pl.ds(0, rim), :],
            send_sem=send_sem.at[0],
            recv_sem=recv_sem.at[0],
            device_id={"tile": tile + 1},
            device_id_type=pl.DeviceIdType.MESH,
        )

    def to_previous():
        return pltpu.make_async_remote_copy(
            src_ref=block_ref.at[half, pl.ds(0, rim), :],
            dst_ref=ext_ref.at[half, pl.ds(rim + size_y, rim), :],
            send_sem=send_sem.at[1],
            recv_sem=recv_sem.at[1],
            device_id={"tile": tile - 1},
            device_id_type=pl.DeviceIdType.MESH,
        )

    def to_mate(start, slot):
        return pltpu.make_async_remote_copy(
            src_ref=ext_ref.at[half, pl.ds(start, rim), :],
            dst_ref=ext_ref.at[half, pl.ds(start, rim), :],
            send_sem=send_sem.at[slot],
            recv_sem=recv_sem.at[slot],
            device_id={"rot": mate},
            device_id_type=pl.DeviceIdType.MESH,
        )

    pl.semaphore_signal(barrier, inc=1, device_id={"rot": mate}, device_id_type=pl.DeviceIdType.MESH)

    @pl.when(before)
    def _():
        pl.semaphore_signal(barrier, inc=1, device_id={"tile": tile - 1}, device_id_type=pl.DeviceIdType.MESH)

    @pl.when(after)
    def _():
        pl.semaphore_signal(barrier, inc=1, device_id={"tile": tile + 1}, device_id_type=pl.DeviceIdType.MESH)

    grid_ref[...] = jnp.zeros(grid_ref.shape, jnp.float32)
    grid_ref[:, :TMPL, :TMPL] = raw_ref[...].astype(jnp.float32)
    shape = grid_ref.shape[1:]
    odd_y = 2 * lax.broadcasted_iota(jnp.int32, shape, 0) - (TMPL - 1)
    odd_z = 2 * lax.broadcasted_iota(jnp.int32, shape, 1) - (TMPL - 1)
    plane_sq = odd_y * odd_y + odd_z * odd_z

    def masked(q, centre):
        odd_x = 2 * q - (TMPL - 1)
        inside = plane_sq + odd_x * odd_x <= TMPL * TMPL
        return jnp.where(inside, grid_ref[q] - centre, 0.0)

    zeros = jnp.zeros(shape, jnp.float32)
    total = lax.fori_loop(0, TMPL, lambda q, held: held + masked(q, 0.0), zeros, unroll=4)
    centre = jnp.sum(total) / voxels

    def add_square(q, held):
        value = masked(q, centre)
        return held + value * value

    squares = jnp.sum(lax.fori_loop(0, TMPL, add_square, zeros, unroll=4), keepdims=True)
    scale = 1.0 / jnp.sqrt(squares / voxels + EPSILON)

    pl.semaphore_wait(barrier, before.astype(jnp.int32) + after.astype(jnp.int32) + 1)

    @pl.when(before)
    def _():
        to_previous().start()

    @pl.when(after)
    def _():
        to_next().start()

    ext_ref[:, rim : rim + size_y, :] = block_ref[...]
    nothing = jnp.zeros((block_ref.shape[0], rim, LANES), jnp.float32)

    @pl.when(jnp.logical_not(before))
    def _():
        ext_ref[:, :rim, :] = nothing

    @pl.when(jnp.logical_not(after))
    def _():
        ext_ref[:, rim + size_y :, :] = nothing

    group = 4

    def step(index, carry):
        pairs = []
        for i in range(group):
            q = 2 * (index * group + i)
            pairs.append(jnp.concatenate([masked(q, centre) * scale, masked(q + 1, centre) * scale], axis=1))
        for which, (re, im) in enumerate(planes(pairs, ly_ref[...], tz_ref[...], length_y)):
            out_ref[2 * group * index + which, :, :LANES] = re
            out_ref[2 * group * index + which, :, LANES:] = im
        return carry

    lax.fori_loop(0, TMPL // (2 * group), step, 0)

    @pl.when(before)
    def _():
        to_previous().wait_send()
        to_next().wait_recv()
        to_mate(0, 2).start()

    @pl.when(after)
    def _():
        to_next().wait_send()
        to_previous().wait_recv()
        to_mate(rim + size_y, 3).start()

    @pl.when(before)
    def _():
        to_mate(0, 2).wait()

    @pl.when(after)
    def _():
        to_mate(rim + size_y, 3).wait()


def exchange_kernel(rots, score_ref, scale_ref, out_ref, others, send_sem, recv_sem):
    me = lax.axis_index("rot")
    rows = scale_ref.shape[0]
    barrier = pltpu.get_barrier_semaphore()
    peers = [lax.rem(me + d, rots) for d in range(1, rots)]
    for peer in peers:
        pl.semaphore_signal(barrier, inc=1, device_id={"rot": peer}, device_id_type=pl.DeviceIdType.MESH)
    pl.semaphore_wait(barrier, rots - 1)
    copies = []
    for d, peer in enumerate(peers):
        copy = pltpu.make_async_remote_copy(
            src_ref=score_ref.at[pl.ds(peer * rows, rows)],
            dst_ref=others.at[d],
            send_sem=send_sem.at[d],
            recv_sem=recv_sem.at[d],
            device_id={"rot": peer},
            device_id_type=pl.DeviceIdType.MESH,
        )
        copy.start()
        copies.append(copy)
    scale = scale_ref[...]
    scores = [score_ref[pl.ds(me * rows, rows)] * scale]
    for copy in copies:
        copy.wait()
    for d in range(rots - 1):
        scores.append(others[d] * scale)
    largest = functools.reduce(jnp.maximum, scores)
    total = functools.reduce(jnp.add, [jnp.exp(score - largest) for score in scores])
    out_ref[...] = largest + jnp.log(total)


def main_kernel(
    dims, places, voxels,
    ext_ref, khat_hbm, mhat_hbm, phase_ref, ly_ref, tz_ref, iy_ref, iz_ref,
    score_ref, scale_ref,
    fields, khat_ref, mhat, stage, mixed, rows, local, sem,
):
    size_in, length_y, padded, size_x, size_y, inner, outer = dims
    length_x = inner * outer
    fetches = [
        pltpu.make_async_copy(khat_hbm, khat_ref, sem.at[0]),
        pltpu.make_async_copy(mhat_hbm, mhat, sem.at[1]),
    ]
    for fetch in fetches:
        fetch.start()
    me = lax.axis_index("rot")

    def forward(step, carry):
        pairs = []
        for i in range(4):
            v = ext_ref[4 * step + i]
            pairs.append(jnp.concatenate([v, v * v], axis=1))
        for which, (re, im) in enumerate(planes(pairs, ly_ref[...], tz_ref[...], length_y)):
            fields[which % 2, 4 * step + which // 2, :, :LANES] = re
            fields[which % 2, 4 * step + which // 2, :, LANES:] = im
        return carry

    lax.fori_loop(0, size_in // 4, forward, 0)
    rows[:, length_y:, :] = jnp.zeros((rows.shape[0], padded - length_y, 2 * LANES), jnp.float32)
    for fetch in fetches:
        fetch.wait()

    def block(r, carry):
        at = pl.ds(pl.multiple_of(r * 8, 8), 8)

        def first(read, slot):
            for n2 in range(inner):
                values = [read(inner * n1 + n2) for n1 in range(outer)]
                for k1, value in enumerate(small_dft(values, -1)):
                    re, im = turn(value, -n2 * k1, length_x)
                    stage[slot, k1 * inner + n2, :, :LANES] = re
                    stage[slot, k1 * inner + n2, :, LANES:] = im

        def field_reader(which):
            def read(n):
                if n >= size_in:
                    return None
                return (fields[which, n, at, :LANES], fields[which, n, at, LANES:])

            return read

        def kernel_reader(n):
            if n not in places:
                return None
            q = places.index(n)
            return (khat_ref[q, at, :LANES], khat_ref[q, at, LANES:])

        first(field_reader(0), 0)
        first(field_reader(1), 1)
        first(kernel_reader, 2)

        def second(slot, k1):
            values = [
                (stage[slot, k1 * inner + n2, :, :LANES], stage[slot, k1 * inner + n2, :, LANES:])
                for n2 in range(inner)
            ]
            return small_dft(values, -1)

        def times(a, b):
            return (a[0] * b[0] + a[1] * b[1], a[1] * b[0] - a[0] * b[1])

        for k1 in range(outer):
            volume = second(0, k1)
            template = second(2, k1)
            mask = [
                (mhat[k1 + outer * k2, at, :LANES], mhat[k1 + outer * k2, at, LANES:])
                for k2 in range(inner)
            ]
            square = second(1, k1)
            products = (
                [times(a, b) for a, b in zip(volume, template)],
                [times(a, b) for a, b in zip(volume, mask)],
                [times(a, b) for a, b in zip(square, mask)],
            )
            for slot, product in enumerate(products):
                for n2, value in enumerate(small_dft(product, 1)):
                    re, im = turn(value, n2 * k1, length_x)
                    mixed[slot, k1 * inner + n2, :, :LANES] = re
                    mixed[slot, k1 * inner + n2, :, LANES:] = im

        for n2 in range(inner):
            def load(slot):
                return [
                    (mixed[slot, k1 * inner + n2, :, :LANES], mixed[slot, k1 * inner + n2, :, LANES:])
                    for k1 in range(outer)
                ]

            sums = small_dft(load(0), 1)
            for n1 in range(size_x // inner):
                rows[inner * n1 + n2, at, :LANES] = sums[n1][0]
                rows[inner * n1 + n2, at, LANES:] = sums[n1][1]
            for slot in (1, 2):
                re_sum = None
                for k1, (re, im) in enumerate(load(slot)):
                    c, s = phase_ref[me, 2 * k1], phase_ref[me, 2 * k1 + 1]
                    re_part, im_part = re * c - im * s, re * s + im * c
                    if re_sum is None:
                        re_sum, im_sum = re_part, im_part
                    else:
                        re_sum, im_sum = re_sum + re_part, im_sum + im_part
                target = size_x + (slot - 1) * inner + n2
                rows[target, at, :LANES] = re_sum
                rows[target, at, LANES:] = im_sum
        return carry

    lax.fori_loop(0, length_y // 8, block, 0)

    group = 8

    def inverse(step, carry):
        flat = []
        for i in range(group):
            o = dot(iy_ref[...], pieces(rows[step * group + i], 0))
            c, s = o[:size_y], o[size_y:]
            re = c[:, :LANES] - s[:, LANES:]
            im = c[:, LANES:] + s[:, :LANES]
            flat.append(jnp.concatenate([re, im], axis=1))
        result = dot(pieces(jnp.concatenate(flat, axis=0), 1), iz_ref[...])
        for i in range(group):
            local[step * group + i] = result[i * size_y : (i + 1) * size_y]
        return carry

    lax.fori_loop(0, (size_x + 2 * inner) // group, inverse, 0)
    score_ref[...] = local[:size_x]
    mean = local[size_x : size_x + inner] / voxels
    square = local[size_x + inner :] / voxels
    std = jnp.sqrt(jnp.maximum(square - mean * mean, VAR_FLOOR))
    scale_ref[...] = SHARPNESS / (math.sqrt(voxels) * std)


def row_halo(block, across):
    tiles = lax.axis_size("tile")
    up = [(t - across, t) for t in range(across, tiles)]
    down = [(t, s) for s, t in up]
    lower = lax.ppermute(block[block.shape[0] - HALF :], "tile", up)
    upper = lax.ppermute(block[:HALF], "tile", down)
    return jnp.concatenate([lower, block, upper], axis=0)


def shards(volume, templates, rot_ids):
    tile_count = lax.axis_size("tile")
    rots = lax.axis_size("rot")
    across = min(tile_count, 8)
    down = tile_count // across
    block = volume[0]
    size_x, size_y, size_z = block.shape
    inner = size_x // rots
    if down > 1:
        block = row_halo(block, across)
        length_x = size_x + TMPL
        places = tuple(range(TMPL))
    else:
        length_x = -(-(size_x + HALF) // (2 * inner)) * 2 * inner
        places = tuple((q - HALF) % length_x for q in range(TMPL))
    outer = length_x // inner
    size_in = block.shape[0]
    length_y = size_y + TMPL
    padded = -(-length_y // 16) * 16
    length_z = size_z + HALF
    freqs = length_z // 2 + 1

    mask = sphere()
    voxels = float(mask.sum())
    rim = -(-HALF // 8) * 8
    reach = size_y + 2 * rim
    tz = jnp.asarray(z_forward(length_z, LANES, freqs))
    kernel_rows = 48
    grid = templates[rot_ids[0]].reshape(TMPL, TMPL, TMPL)
    vmem = pl.BlockSpec(memory_space=pltpu.VMEM)
    khat, extended = pl.pallas_call(
        functools.partial(template_kernel, length_y, across, rim, voxels),
        out_shape=(
            jax.ShapeDtypeStruct((TMPL, length_y, 2 * LANES), jnp.float32),
            jax.ShapeDtypeStruct((size_in, reach, size_z), jnp.float32),
        ),
        in_specs=[vmem] * 4,
        out_specs=(vmem, vmem),
        scratch_shapes=[
            pltpu.VMEM((TMPL, kernel_rows, LANES), jnp.float32),
            pltpu.SemaphoreType.DMA((4,)),
            pltpu.SemaphoreType.DMA((4,)),
        ],
        compiler_params=pltpu.CompilerParams(vmem_limit_bytes=VMEM, collective_id=0, has_side_effects=True),
        name="template_spectrum",
    )(grid, block, jnp.asarray(y_forward(length_y, kernel_rows, 0)), tz)

    mhat = jnp.asarray(mask_spectrum(places, length_x, length_y, length_z, freqs))
    turns = angles(outer, np.arange(rots), np.arange(outer))
    phase = jnp.asarray(np.stack([np.cos(turns), np.sin(turns)], axis=2).reshape(rots, 2 * outer).astype(np.float32))
    dims = (size_in, length_y, padded, size_x, size_y, inner, outer)
    scores, scale = pl.pallas_call(
        functools.partial(main_kernel, dims, places, voxels),
        out_shape=(
            jax.ShapeDtypeStruct((size_x, size_y, size_z), jnp.float32),
            jax.ShapeDtypeStruct((inner, size_y, size_z), jnp.float32),
        ),
        in_specs=[
            vmem, pl.BlockSpec(memory_space=pl.ANY), pl.BlockSpec(memory_space=pl.ANY), pl.BlockSpec(memory_space=pltpu.SMEM),
            vmem, vmem, vmem, vmem,
        ],
        out_specs=(vmem, vmem),
        scratch_shapes=[
            pltpu.VMEM((2, size_in, length_y, 2 * LANES), jnp.float32),
            pltpu.VMEM((TMPL, length_y, 2 * LANES), jnp.float32),
            pltpu.VMEM((length_x, length_y, 2 * LANES), jnp.float32),
            pltpu.VMEM((3, length_x, 8, 2 * LANES), jnp.float32),
            pltpu.VMEM((3, length_x, 8, 2 * LANES), jnp.float32),
            pltpu.VMEM((size_x + 2 * inner, padded, 2 * LANES), jnp.float32),
            pltpu.VMEM((size_x + 2 * inner, size_y, size_z), jnp.float32),
            pltpu.SemaphoreType.DMA((2,)),
        ],
        compiler_params=pltpu.CompilerParams(vmem_limit_bytes=VMEM),
        name="correlate",
    )(
        extended, khat, mhat, phase,
        jnp.asarray(y_forward(length_y, reach, rim - HALF)), tz,
        jnp.asarray(y_inverse(length_y, padded, size_y)),
        jnp.asarray(z_inverse(length_z, size_z, freqs, length_x)),
    )
    result = pl.pallas_call(
        functools.partial(exchange_kernel, rots),
        out_shape=jax.ShapeDtypeStruct((inner, size_y, size_z), jnp.float32),
        in_specs=[vmem, vmem],
        out_specs=vmem,
        scratch_shapes=[
            pltpu.VMEM((rots - 1, inner, size_y, size_z), jnp.float32),
            pltpu.SemaphoreType.DMA((rots - 1,)),
            pltpu.SemaphoreType.DMA((rots - 1,)),
        ],
        compiler_params=pltpu.CompilerParams(vmem_limit_bytes=VMEM, collective_id=1, has_side_effects=True),
        name="exchange",
    )(scores, scale)
    return result[None]


def solution(mesh):
    return jax.shard_map(
        shards,
        mesh=mesh,
        in_specs=(P("tile", None, None, None), P(), P("rot")),
        out_specs=P("tile", "rot", None, None),
        check_vma=False,
    )
```

```python
import functools
import math

import jax
import jax.numpy as jnp
import ml_dtypes
import numpy as np
from jax import lax
from jax.experimental import pallas as pl
from jax.experimental.pallas import tpu as pltpu
from jax.sharding import PartitionSpec as P

TMPL = 40
HALF = TMPL // 2
VAR_FLOOR = 0.05
EPSILON = 1e-06
SHARPNESS = 2.0
LANES = 128
VMEM = 56 * 1024 * 1024


def sphere():
    offsets = np.arange(TMPL) - (TMPL - 1) / 2.0
    squares = offsets**2
    radius_sq = squares[:, None, None] + squares[None, :, None] + squares[None, None, :]
    return (radius_sq <= (TMPL / 2.0) ** 2).astype(np.float64)


def halves(table):
    high = table.astype(ml_dtypes.bfloat16)
    low = (table - high.astype(np.float64)).astype(ml_dtypes.bfloat16)
    return high, low


def left_table(table):
    high, low = halves(table)
    return np.concatenate([high, high, low], axis=1)


def right_table(table):
    high, low = halves(table)
    return np.concatenate([high, high, low], axis=0)


def wide(table, axis, size):
    pad = [(0, 0), (0, 0)]
    pad[axis] = (0, size - table.shape[axis])
    return np.pad(table, pad)


def angles(length, rows, columns):
    return 2.0 * math.pi * ((np.asarray(rows)[:, None] * np.asarray(columns)[None, :]) % length) / length


def y_forward(length, inputs, offset):
    y = np.arange(inputs) - offset
    theta = angles(length, np.arange(length), y)
    inside = ((y >= 0) & (y < length))[None, :]
    return left_table(np.concatenate([np.cos(theta) * inside, np.sin(theta) * inside], axis=0))


def z_forward(length, inputs, freqs):
    theta = angles(length, np.arange(inputs), np.arange(freqs))
    return right_table(np.concatenate([wide(np.cos(theta), 1, LANES), wide(np.sin(theta), 1, LANES)], axis=1))


def y_inverse(length, padded, outputs):
    theta = angles(length, np.arange(outputs), np.arange(length))
    both = np.concatenate([np.cos(theta), np.sin(theta)], axis=0) / length
    return left_table(wide(both, 1, padded))


def z_inverse(length, outputs, freqs, extra):
    theta = angles(length, np.arange(freqs), np.arange(outputs) - HALF)
    index = np.arange(freqs)
    weight = np.where((index == 0) | (2 * index == length), 1.0, 2.0)[:, None] / (length * extra)
    real = wide(np.cos(theta) * weight, 0, LANES)
    imag = wide(-np.sin(theta) * weight, 0, LANES)
    return right_table(np.concatenate([real, imag], axis=0))


def mask_spectrum(places, length_x, length_y, length_z, freqs):
    field = np.zeros((length_x, length_y, length_z))
    field[np.asarray(places), :TMPL, :TMPL] = sphere()
    spec = np.fft.rfftn(field)
    gap = ((0, 0), (0, 0), (0, LANES - freqs))
    return np.concatenate([np.pad(spec.real, gap), np.pad(spec.imag, gap)], axis=2).astype(np.float32)


def plus(a, b):
    if a is None:
        return b
    if b is None:
        return a
    return (a[0] + b[0], a[1] + b[1])


def minus(a, b):
    if b is None:
        return a
    if a is None:
        return (-b[0], -b[1])
    return (a[0] - b[0], a[1] - b[1])


def turn(a, step, length):
    if a is None:
        return None
    step %= length
    re, im = a
    eighth = 8 * step
    if eighth % length == 0:
        part = eighth // length
        root = math.sqrt(0.5)
        if part == 0:
            return a
        if part == 2:
            return (-im, re)
        if part == 4:
            return (-re, -im)
        if part == 6:
            return (im, -re)
        if part == 1:
            return ((re - im) * root, (re + im) * root)
        if part == 3:
            return ((re + im) * -root, (re - im) * root)
        if part == 5:
            return ((im - re) * root, (re + im) * -root)
        return ((re + im) * root, (im - re) * root)
    c = math.cos(2.0 * math.pi * step / length)
    s = math.sin(2.0 * math.pi * step / length)
    return (re * c - im * s, re * s + im * c)


def small_dft(values, sign):
    length = len(values)
    if length == 1:
        return values
    if length % 2 == 0:
        even = small_dft(values[0::2], sign)
        odd = small_dft(values[1::2], sign)
        odd = [turn(value, sign * k, length) for k, value in enumerate(odd)]
        return [plus(e, o) for e, o in zip(even, odd)] + [minus(e, o) for e, o in zip(even, odd)]
    sums = []
    for k in range(length):
        total = None
        for n in range(length):
            total = plus(total, turn(values[n], sign * n * k, length))
        sums.append(total)
    return sums


def pieces(values, axis):
    high = values.astype(jnp.bfloat16)
    low = (values - high.astype(jnp.float32)).astype(jnp.bfloat16)
    return jnp.concatenate([high, low, high], axis=axis)


def dot(a, b):
    return jnp.dot(a, b, preferred_element_type=jnp.float32)


def planes(pairs, ly, tz, length_y):
    flat = []
    for pair in pairs:
        o = dot(ly, pieces(pair, 0))
        flat += [o[:, :LANES], o[:, LANES:]]
    h = dot(pieces(jnp.concatenate(flat, axis=0), 1), tz)
    outs = []
    for which in range(2 * len(pairs)):
        base = 2 * length_y * which
        c = h[base : base + length_y]
        s = h[base + length_y : base + 2 * length_y]
        outs.append((c[:, :LANES] - s[:, LANES:], -s[:, :LANES] - c[:, LANES:]))
    return outs


def template_kernel(
    length_y, across, rim, voxels, raw_ref, block_ref, ly_ref, tz_ref, out_ref, ext_ref,
    grid_ref, send_sem, recv_sem,
):
    tile = lax.axis_index("tile")
    core = lax.rem(lax.axis_index("rot"), 2)
    mate = lax.axis_index("rot") + 1 - 2 * core
    depth = block_ref.shape[0] // 2
    half = pl.ds(core * depth, depth)
    column = lax.rem(tile, across)
    before, after = column > 0, column < across - 1
    size_y = block_ref.shape[1]
    barrier = pltpu.get_barrier_semaphore()

    def to_next():
        return pltpu.make_async_remote_copy(
            src_ref=block_ref.at[half, pl.ds(size_y - rim, rim), :],
            dst_ref=ext_ref.at[half, pl.ds(0, rim), :],
            send_sem=send_sem.at[0],
            recv_sem=recv_sem.at[0],
            device_id={"tile": tile + 1},
            device_id_type=pl.DeviceIdType.MESH,
        )

    def to_previous():
        return pltpu.make_async_remote_copy(
            src_ref=block_ref.at[half, pl.ds(0, rim), :],
            dst_ref=ext_ref.at[half, pl.ds(rim + size_y, rim), :],
            send_sem=send_sem.at[1],
            recv_sem=recv_sem.at[1],
            device_id={"tile": tile - 1},
            device_id_type=pl.DeviceIdType.MESH,
        )

    def to_mate(start, slot):
        return pltpu.make_async_remote_copy(
            src_ref=ext_ref.at[half, pl.ds(start, rim), :],
            dst_ref=ext_ref.at[half, pl.ds(start, rim), :],
            send_sem=send_sem.at[slot],
            recv_sem=recv_sem.at[slot],
            device_id={"rot": mate},
            device_id_type=pl.DeviceIdType.MESH,
        )

    pl.semaphore_signal(barrier, inc=1, device_id={"rot": mate}, device_id_type=pl.DeviceIdType.MESH)

    @pl.when(before)
    def _():
        pl.semaphore_signal(barrier, inc=1, device_id={"tile": tile - 1}, device_id_type=pl.DeviceIdType.MESH)

    @pl.when(after)
    def _():
        pl.semaphore_signal(barrier, inc=1, device_id={"tile": tile + 1}, device_id_type=pl.DeviceIdType.MESH)

    pl.semaphore_wait(barrier, before.astype(jnp.int32) + after.astype(jnp.int32) + 1)

    @pl.when(before)
    def _():
        to_previous().start()

    @pl.when(after)
    def _():
        to_next().start()

    grid_ref[...] = jnp.zeros(grid_ref.shape, jnp.float32)
    grid_ref[:, :TMPL, :TMPL] = raw_ref[...].astype(jnp.float32)
    shape = grid_ref.shape[1:]
    odd_y = 2 * lax.broadcasted_iota(jnp.int32, shape, 0) - (TMPL - 1)
    odd_z = 2 * lax.broadcasted_iota(jnp.int32, shape, 1) - (TMPL - 1)
    plane_sq = odd_y * odd_y + odd_z * odd_z

    def masked(q, centre):
        odd_x = 2 * q - (TMPL - 1)
        inside = plane_sq + odd_x * odd_x <= TMPL * TMPL
        return jnp.where(inside, grid_ref[q] - centre, 0.0)

    zeros = jnp.zeros(shape, jnp.float32)
    total = lax.fori_loop(0, TMPL, lambda q, held: held + masked(q, 0.0), zeros, unroll=4)
    centre = jnp.sum(total) / voxels

    def add_square(q, held):
        value = masked(q, centre)
        return held + value * value

    squares = jnp.sum(lax.fori_loop(0, TMPL, add_square, zeros, unroll=4), keepdims=True)
    scale = 1.0 / jnp.sqrt(squares / voxels + EPSILON)

    ext_ref[:, rim : rim + size_y, :] = block_ref[...]
    nothing = jnp.zeros((block_ref.shape[0], rim, LANES), jnp.float32)

    @pl.when(jnp.logical_not(before))
    def _():
        ext_ref[:, :rim, :] = nothing

    @pl.when(jnp.logical_not(after))
    def _():
        ext_ref[:, rim + size_y :, :] = nothing

    group = 4

    def step(index, carry):
        pairs = []
        for i in range(group):
            q = 2 * (index * group + i)
            pairs.append(jnp.concatenate([masked(q, centre) * scale, masked(q + 1, centre) * scale], axis=1))
        for which, (re, im) in enumerate(planes(pairs, ly_ref[...], tz_ref[...], length_y)):
            out_ref[2 * group * index + which, :, :LANES] = re
            out_ref[2 * group * index + which, :, LANES:] = im
        return carry

    lax.fori_loop(0, TMPL // (2 * group), step, 0)

    @pl.when(before)
    def _():
        to_previous().wait_send()
        to_next().wait_recv()
        to_mate(0, 2).start()

    @pl.when(after)
    def _():
        to_next().wait_send()
        to_previous().wait_recv()
        to_mate(rim + size_y, 3).start()

    @pl.when(before)
    def _():
        to_mate(0, 2).wait()

    @pl.when(after)
    def _():
        to_mate(rim + size_y, 3).wait()


def main_kernel(
    dims, places, voxels,
    ext_ref, khat_hbm, mhat_hbm, phase_ref, ly_ref, tz_ref, iy_ref, iz_ref,
    largest_ref, total_ref,
    fields, khat_ref, mhat, stage, mixed, rows, local, others, sem, send_sem, recv_sem,
):
    size_in, length_y, padded, size_x, size_y, inner, outer = dims
    length_x = inner * outer
    fetches = [
        pltpu.make_async_copy(khat_hbm, khat_ref, sem.at[0]),
        pltpu.make_async_copy(mhat_hbm, mhat, sem.at[1]),
    ]
    for fetch in fetches:
        fetch.start()
    me = lax.axis_index("rot")
    rots = size_x // inner
    mate = me + 1 - 2 * lax.rem(me, 2)
    peers = (lax.rem(me + 2, rots), lax.rem(mate + 2, rots), mate)
    barrier = pltpu.get_barrier_semaphore()
    for peer in peers:
        pl.semaphore_signal(barrier, inc=1, device_id={"rot": peer}, device_id_type=pl.DeviceIdType.MESH)

    def forward(step, carry):
        pairs = []
        for i in range(4):
            v = ext_ref[4 * step + i]
            pairs.append(jnp.concatenate([v, v * v], axis=1))
        for which, (re, im) in enumerate(planes(pairs, ly_ref[...], tz_ref[...], length_y)):
            fields[which % 2, 4 * step + which // 2, :, :LANES] = re
            fields[which % 2, 4 * step + which // 2, :, LANES:] = im
        return carry

    lax.fori_loop(0, size_in // 4, forward, 0)
    rows[:, length_y:, :] = jnp.zeros((rows.shape[0], padded - length_y, 2 * LANES), jnp.float32)
    for fetch in fetches:
        fetch.wait()

    def block(r, carry):
        at = pl.ds(pl.multiple_of(r * 8, 8), 8)

        def first(read, slot):
            for n2 in range(inner):
                values = [read(inner * n1 + n2) for n1 in range(outer)]
                for k1, value in enumerate(small_dft(values, -1)):
                    re, im = turn(value, -n2 * k1, length_x)
                    stage[slot, k1 * inner + n2, :, :LANES] = re
                    stage[slot, k1 * inner + n2, :, LANES:] = im

        def field_reader(which):
            def read(n):
                if n >= size_in:
                    return None
                return (fields[which, n, at, :LANES], fields[which, n, at, LANES:])

            return read

        def kernel_reader(n):
            if n not in places:
                return None
            q = places.index(n)
            return (khat_ref[q, at, :LANES], khat_ref[q, at, LANES:])

        first(field_reader(0), 0)
        first(field_reader(1), 1)
        first(kernel_reader, 2)

        def second(slot, k1):
            values = [
                (stage[slot, k1 * inner + n2, :, :LANES], stage[slot, k1 * inner + n2, :, LANES:])
                for n2 in range(inner)
            ]
            return small_dft(values, -1)

        def times(a, b):
            return (a[0] * b[0] + a[1] * b[1], a[1] * b[0] - a[0] * b[1])

        for k1 in range(outer):
            volume = second(0, k1)
            template = second(2, k1)
            mask = [
                (mhat[k1 + outer * k2, at, :LANES], mhat[k1 + outer * k2, at, LANES:])
                for k2 in range(inner)
            ]
            square = second(1, k1)
            products = (
                [times(a, b) for a, b in zip(volume, template)],
                [times(a, b) for a, b in zip(volume, mask)],
                [times(a, b) for a, b in zip(square, mask)],
            )
            for slot, product in enumerate(products):
                for n2, value in enumerate(small_dft(product, 1)):
                    re, im = turn(value, n2 * k1, length_x)
                    mixed[slot, k1 * inner + n2, :, :LANES] = re
                    mixed[slot, k1 * inner + n2, :, LANES:] = im

        for n2 in range(inner):
            def load(slot):
                return [
                    (mixed[slot, k1 * inner + n2, :, :LANES], mixed[slot, k1 * inner + n2, :, LANES:])
                    for k1 in range(outer)
                ]

            sums = small_dft(load(0), 1)
            for n1 in range(size_x // inner):
                rows[inner * n1 + n2, at, :LANES] = sums[n1][0]
                rows[inner * n1 + n2, at, LANES:] = sums[n1][1]
            for slot in (1, 2):
                re_sum = None
                for k1, (re, im) in enumerate(load(slot)):
                    c, s = phase_ref[me, 2 * k1], phase_ref[me, 2 * k1 + 1]
                    re_part, im_part = re * c - im * s, re * s + im * c
                    if re_sum is None:
                        re_sum, im_sum = re_part, im_part
                    else:
                        re_sum, im_sum = re_sum + re_part, im_sum + im_part
                target = size_x + (slot - 1) * inner + n2
                rows[target, at, :LANES] = re_sum
                rows[target, at, LANES:] = im_sum
        return carry

    lax.fori_loop(0, length_y // 8, block, 0)

    def inverse(part):
        flat = []
        for i in range(inner):
            o = dot(iy_ref[...], pieces(rows[part * inner + i], 0))
            c, s = o[:size_y], o[size_y:]
            re = c[:, :LANES] - s[:, LANES:]
            im = c[:, LANES:] + s[:, :LANES]
            flat.append(jnp.concatenate([re, im], axis=1))
        result = dot(pieces(jnp.concatenate(flat, axis=0), 1), iz_ref[...])
        return result.reshape(inner, size_y, LANES)

    pl.semaphore_wait(barrier, len(peers))
    copies = []
    for slot, peer in enumerate(peers):
        local[slot] = inverse(peer)
        copy = pltpu.make_async_remote_copy(
            src_ref=local.at[slot],
            dst_ref=others.at[slot],
            send_sem=send_sem.at[slot],
            recv_sem=recv_sem.at[slot],
            device_id={"rot": peer},
            device_id_type=pl.DeviceIdType.MESH,
        )
        copy.start()
        copies.append(copy)
    mean = inverse(rots) / voxels
    square = inverse(rots + 1) / voxels
    std = jnp.sqrt(jnp.maximum(square - mean * mean, VAR_FLOOR))
    scale = SHARPNESS / (math.sqrt(voxels) * std)
    scores = [inverse(me) * scale]
    for copy in copies:
        copy.wait()
    for slot in range(len(peers)):
        scores.append(others[slot] * scale)
    largest = functools.reduce(jnp.maximum, scores)
    largest_ref[...] = largest
    total_ref[...] = functools.reduce(jnp.add, [jnp.exp(score - largest) for score in scores])


def row_halo(block, across):
    tiles = lax.axis_size("tile")
    up = [(t - across, t) for t in range(across, tiles)]
    down = [(t, s) for s, t in up]
    lower = lax.ppermute(block[block.shape[0] - HALF :], "tile", up)
    upper = lax.ppermute(block[:HALF], "tile", down)
    return jnp.concatenate([lower, block, upper], axis=0)


def shards(volume, templates, rot_ids):
    tile_count = lax.axis_size("tile")
    rots = lax.axis_size("rot")
    across = min(tile_count, 8)
    down = tile_count // across
    block = volume[0]
    size_x, size_y, size_z = block.shape
    inner = size_x // rots
    if down > 1:
        block = row_halo(block, across)
        length_x = size_x + TMPL
        places = tuple(range(TMPL))
    else:
        length_x = -(-(size_x + HALF) // (2 * inner)) * 2 * inner
        places = tuple((q - HALF) % length_x for q in range(TMPL))
    outer = length_x // inner
    size_in = block.shape[0]
    length_y = size_y + TMPL
    padded = -(-length_y // 16) * 16
    length_z = size_z + HALF
    freqs = length_z // 2 + 1

    mask = sphere()
    voxels = float(mask.sum())
    rim = -(-HALF // 8) * 8
    reach = size_y + 2 * rim
    tz = jnp.asarray(z_forward(length_z, LANES, freqs))
    kernel_rows = 48
    grid = templates[rot_ids[0]].reshape(TMPL, TMPL, TMPL)
    vmem = pl.BlockSpec(memory_space=pltpu.VMEM)
    khat, extended = pl.pallas_call(
        functools.partial(template_kernel, length_y, across, rim, voxels),
        out_shape=(
            jax.ShapeDtypeStruct((TMPL, length_y, 2 * LANES), jnp.float32),
            jax.ShapeDtypeStruct((size_in, reach, size_z), jnp.float32),
        ),
        in_specs=[vmem] * 4,
        out_specs=(vmem, vmem),
        scratch_shapes=[
            pltpu.VMEM((TMPL, kernel_rows, LANES), jnp.float32),
            pltpu.SemaphoreType.DMA((4,)),
            pltpu.SemaphoreType.DMA((4,)),
        ],
        compiler_params=pltpu.CompilerParams(vmem_limit_bytes=VMEM, collective_id=0, has_side_effects=True),
        name="template_spectrum",
    )(grid, block, jnp.asarray(y_forward(length_y, kernel_rows, 0)), tz)

    mhat = jnp.asarray(mask_spectrum(places, length_x, length_y, length_z, freqs))
    turns = angles(outer, np.arange(rots), np.arange(outer))
    phase = jnp.asarray(np.stack([np.cos(turns), np.sin(turns)], axis=2).reshape(rots, 2 * outer).astype(np.float32))
    dims = (size_in, length_y, padded, size_x, size_y, inner, outer)
    largest, total = pl.pallas_call(
        functools.partial(main_kernel, dims, places, voxels),
        out_shape=(
            jax.ShapeDtypeStruct((inner, size_y, size_z), jnp.float32),
            jax.ShapeDtypeStruct((inner, size_y, size_z), jnp.float32),
        ),
        in_specs=[
            vmem, pl.BlockSpec(memory_space=pl.ANY), pl.BlockSpec(memory_space=pl.ANY), pl.BlockSpec(memory_space=pltpu.SMEM),
            vmem, vmem, vmem, vmem,
        ],
        out_specs=(vmem, vmem),
        scratch_shapes=[
            pltpu.VMEM((2, size_in, length_y, 2 * LANES), jnp.float32),
            pltpu.VMEM((TMPL, length_y, 2 * LANES), jnp.float32),
            pltpu.VMEM((length_x, length_y, 2 * LANES), jnp.float32),
            pltpu.VMEM((3, length_x, 8, 2 * LANES), jnp.float32),
            pltpu.VMEM((3, length_x, 8, 2 * LANES), jnp.float32),
            pltpu.VMEM((size_x + 2 * inner, padded, 2 * LANES), jnp.float32),
            pltpu.VMEM((rots - 1, inner, size_y, size_z), jnp.float32),
            pltpu.VMEM((rots - 1, inner, size_y, size_z), jnp.float32),
            pltpu.SemaphoreType.DMA((2,)),
            pltpu.SemaphoreType.DMA((rots - 1,)),
            pltpu.SemaphoreType.DMA((rots - 1,)),
        ],
        compiler_params=pltpu.CompilerParams(vmem_limit_bytes=VMEM, collective_id=1, has_side_effects=True),
        name="correlate",
    )(
        extended, khat, mhat, phase,
        jnp.asarray(y_forward(length_y, reach, rim - HALF)), tz,
        jnp.asarray(y_inverse(length_y, padded, size_y)),
        jnp.asarray(z_inverse(length_z, size_z, freqs, length_x)),
    )
    return (largest + jnp.log(total))[None]


def solution(mesh):
    return jax.shard_map(
        shards,
        mesh=mesh,
        in_specs=(P("tile", None, None, None), P(), P("rot")),
        out_specs=P("tile", "rot", None, None),
        check_vma=False,
    )
```

```python
import functools
import math

import jax
import jax.numpy as jnp
import ml_dtypes
import numpy as np
from jax import lax
from jax.experimental import pallas as pl
from jax.experimental.pallas import tpu as pltpu
from jax.sharding import PartitionSpec as P

TMPL = 40
HALF = TMPL // 2
VAR_FLOOR = 0.05
EPSILON = 1e-06
SHARPNESS = 2.0
LANES = 128
VMEM = 56 * 1024 * 1024


def sphere():
    offsets = np.arange(TMPL) - (TMPL - 1) / 2.0
    squares = offsets**2
    radius_sq = squares[:, None, None] + squares[None, :, None] + squares[None, None, :]
    return (radius_sq <= (TMPL / 2.0) ** 2).astype(np.float64)


def halves(table):
    high = table.astype(ml_dtypes.bfloat16)
    low = (table - high.astype(np.float64)).astype(ml_dtypes.bfloat16)
    return high, low


def left_table(table):
    high, low = halves(table)
    return np.concatenate([high, high, low], axis=1)


def right_table(table):
    high, low = halves(table)
    return np.concatenate([high, high, low], axis=0)


def wide(table, axis, size):
    pad = [(0, 0), (0, 0)]
    pad[axis] = (0, size - table.shape[axis])
    return np.pad(table, pad)


def angles(length, rows, columns):
    return 2.0 * math.pi * ((np.asarray(rows)[:, None] * np.asarray(columns)[None, :]) % length) / length


def y_forward(length, inputs, offset):
    y = np.arange(inputs) - offset
    theta = angles(length, np.arange(length), y)
    inside = ((y >= 0) & (y < length))[None, :]
    return left_table(np.concatenate([np.cos(theta) * inside, np.sin(theta) * inside], axis=0))


def z_forward(length, inputs, freqs):
    theta = angles(length, np.arange(inputs), np.arange(freqs))
    return right_table(np.concatenate([wide(np.cos(theta), 1, LANES), wide(np.sin(theta), 1, LANES)], axis=1))


def y_inverse(length, padded, outputs):
    theta = angles(length, np.arange(outputs), np.arange(length))
    both = np.concatenate([np.cos(theta), np.sin(theta)], axis=0) / length
    return left_table(wide(both, 1, padded))


def z_inverse(length, outputs, freqs, extra):
    theta = angles(length, np.arange(freqs), np.arange(outputs) - HALF)
    index = np.arange(freqs)
    weight = np.where((index == 0) | (2 * index == length), 1.0, 2.0)[:, None] / (length * extra)
    real = wide(np.cos(theta) * weight, 0, LANES)
    imag = wide(-np.sin(theta) * weight, 0, LANES)
    return right_table(np.concatenate([real, imag], axis=0))


def mask_spectrum(places, length_x, length_y, length_z, freqs):
    field = np.zeros((length_x, length_y, length_z))
    field[np.asarray(places), :TMPL, :TMPL] = sphere()
    spec = np.fft.rfftn(field)
    gap = ((0, 0), (0, 0), (0, LANES - freqs))
    return np.concatenate([np.pad(spec.real, gap), np.pad(spec.imag, gap)], axis=2).astype(np.float32)


def plus(a, b):
    if a is None:
        return b
    if b is None:
        return a
    return (a[0] + b[0], a[1] + b[1])


def minus(a, b):
    if b is None:
        return a
    if a is None:
        return (-b[0], -b[1])
    return (a[0] - b[0], a[1] - b[1])


def turn(a, step, length):
    if a is None:
        return None
    step %= length
    re, im = a
    eighth = 8 * step
    if eighth % length == 0:
        part = eighth // length
        root = math.sqrt(0.5)
        if part == 0:
            return a
        if part == 2:
            return (-im, re)
        if part == 4:
            return (-re, -im)
        if part == 6:
            return (im, -re)
        if part == 1:
            return ((re - im) * root, (re + im) * root)
        if part == 3:
            return ((re + im) * -root, (re - im) * root)
        if part == 5:
            return ((im - re) * root, (re + im) * -root)
        return ((re + im) * root, (im - re) * root)
    c = math.cos(2.0 * math.pi * step / length)
    s = math.sin(2.0 * math.pi * step / length)
    return (re * c - im * s, re * s + im * c)


def small_dft(values, sign):
    length = len(values)
    if length == 1:
        return values
    if length % 2 == 0:
        even = small_dft(values[0::2], sign)
        odd = small_dft(values[1::2], sign)
        odd = [turn(value, sign * k, length) for k, value in enumerate(odd)]
        return [plus(e, o) for e, o in zip(even, odd)] + [minus(e, o) for e, o in zip(even, odd)]
    sums = []
    for k in range(length):
        total = None
        for n in range(length):
            total = plus(total, turn(values[n], sign * n * k, length))
        sums.append(total)
    return sums


def pieces(values, axis):
    high = values.astype(jnp.bfloat16)
    low = (values - high.astype(jnp.float32)).astype(jnp.bfloat16)
    return jnp.concatenate([high, low, high], axis=axis)


def dot(a, b):
    return jnp.dot(a, b, preferred_element_type=jnp.float32)


def planes(pairs, ly, tz, length_y):
    flat = []
    for pair in pairs:
        o = dot(ly, pieces(pair, 0))
        flat += [o[:, :LANES], o[:, LANES:]]
    h = dot(pieces(jnp.concatenate(flat, axis=0), 1), tz)
    outs = []
    for which in range(2 * len(pairs)):
        base = 2 * length_y * which
        c = h[base : base + length_y]
        s = h[base + length_y : base + 2 * length_y]
        outs.append((c[:, :LANES] - s[:, LANES:], -s[:, :LANES] - c[:, LANES:]))
    return outs


def halo_and_template(
    length_y, across, rim, voxels, raw_ref, block_ref, ly_ref, tz_ref, out_ref, ext_ref,
    grid_ref, send_sem, recv_sem, peers,
):
    tile = lax.axis_index("tile")
    core = lax.rem(lax.axis_index("rot"), 2)
    mate = lax.axis_index("rot") + 1 - 2 * core
    depth = block_ref.shape[0] // 2
    half = pl.ds(core * depth, depth)
    column = lax.rem(tile, across)
    before, after = column > 0, column < across - 1
    size_y = block_ref.shape[1]
    barrier = pltpu.get_barrier_semaphore()

    def to_next():
        return pltpu.make_async_remote_copy(
            src_ref=block_ref.at[half, pl.ds(size_y - rim, rim), :],
            dst_ref=ext_ref.at[half, pl.ds(0, rim), :],
            send_sem=send_sem.at[0],
            recv_sem=recv_sem.at[0],
            device_id={"tile": tile + 1},
            device_id_type=pl.DeviceIdType.MESH,
        )

    def to_previous():
        return pltpu.make_async_remote_copy(
            src_ref=block_ref.at[half, pl.ds(0, rim), :],
            dst_ref=ext_ref.at[half, pl.ds(rim + size_y, rim), :],
            send_sem=send_sem.at[1],
            recv_sem=recv_sem.at[1],
            device_id={"tile": tile - 1},
            device_id_type=pl.DeviceIdType.MESH,
        )

    def to_mate(start, slot):
        return pltpu.make_async_remote_copy(
            src_ref=ext_ref.at[half, pl.ds(start, rim), :],
            dst_ref=ext_ref.at[half, pl.ds(start, rim), :],
            send_sem=send_sem.at[slot],
            recv_sem=recv_sem.at[slot],
            device_id={"rot": mate},
            device_id_type=pl.DeviceIdType.MESH,
        )

    for peer in peers:
        pl.semaphore_signal(barrier, inc=1, device_id={"rot": peer}, device_id_type=pl.DeviceIdType.MESH)

    @pl.when(before)
    def _():
        pl.semaphore_signal(barrier, inc=1, device_id={"tile": tile - 1}, device_id_type=pl.DeviceIdType.MESH)

    @pl.when(after)
    def _():
        pl.semaphore_signal(barrier, inc=1, device_id={"tile": tile + 1}, device_id_type=pl.DeviceIdType.MESH)

    pl.semaphore_wait(barrier, before.astype(jnp.int32) + after.astype(jnp.int32) + len(peers))

    @pl.when(before)
    def _():
        to_previous().start()

    @pl.when(after)
    def _():
        to_next().start()

    grid_ref[...] = jnp.zeros(grid_ref.shape, jnp.float32)
    grid_ref[:, :TMPL, :TMPL] = raw_ref[...].astype(jnp.float32)
    shape = grid_ref.shape[1:]
    odd_y = 2 * lax.broadcasted_iota(jnp.int32, shape, 0) - (TMPL - 1)
    odd_z = 2 * lax.broadcasted_iota(jnp.int32, shape, 1) - (TMPL - 1)
    plane_sq = odd_y * odd_y + odd_z * odd_z

    def masked(q, centre):
        odd_x = 2 * q - (TMPL - 1)
        inside = plane_sq + odd_x * odd_x <= TMPL * TMPL
        return jnp.where(inside, grid_ref[q] - centre, 0.0)

    zeros = jnp.zeros(shape, jnp.float32)
    total = lax.fori_loop(0, TMPL, lambda q, held: held + masked(q, 0.0), zeros, unroll=4)
    centre = jnp.sum(total) / voxels

    def add_square(q, held):
        value = masked(q, centre)
        return held + value * value

    squares = jnp.sum(lax.fori_loop(0, TMPL, add_square, zeros, unroll=4), keepdims=True)
    scale = 1.0 / jnp.sqrt(squares / voxels + EPSILON)

    ext_ref[:, rim : rim + size_y, :] = block_ref[...]
    nothing = jnp.zeros((block_ref.shape[0], rim, LANES), jnp.float32)

    @pl.when(jnp.logical_not(before))
    def _():
        ext_ref[:, :rim, :] = nothing

    @pl.when(jnp.logical_not(after))
    def _():
        ext_ref[:, rim + size_y :, :] = nothing

    group = 4

    def step(index, carry):
        pairs = []
        for i in range(group):
            q = 2 * (index * group + i)
            pairs.append(jnp.concatenate([masked(q, centre) * scale, masked(q + 1, centre) * scale], axis=1))
        for which, (re, im) in enumerate(planes(pairs, ly_ref[...], tz_ref[...], length_y)):
            out_ref[2 * group * index + which, :, :LANES] = re
            out_ref[2 * group * index + which, :, LANES:] = im
        return carry

    lax.fori_loop(0, TMPL // (2 * group), step, 0)

    @pl.when(before)
    def _():
        to_previous().wait_send()
        to_next().wait_recv()
        to_mate(0, 2).start()

    @pl.when(after)
    def _():
        to_next().wait_send()
        to_previous().wait_recv()
        to_mate(rim + size_y, 3).start()

    @pl.when(before)
    def _():
        to_mate(0, 2).wait()

    @pl.when(after)
    def _():
        to_mate(rim + size_y, 3).wait()


def main_kernel(
    dims, places, voxels,
    raw_ref, block_ref, mhat_hbm, phase_ref, lk_ref, ly_ref, tz_ref, iy_ref, iz_ref,
    largest_ref, total_ref,
    grid_ref, ext_ref, fields, khat_ref, mhat, stage, mixed, rows, local, others,
    sem, rim_send, rim_recv, send_sem, recv_sem,
):
    size_in, length_y, padded, size_x, size_y, inner, outer, across, rim = dims
    length_x = inner * outer
    fetch = pltpu.make_async_copy(mhat_hbm, mhat, sem)
    fetch.start()
    me = lax.axis_index("rot")
    rots = size_x // inner
    mate = me + 1 - 2 * lax.rem(me, 2)
    peers = (lax.rem(me + 2, rots), lax.rem(mate + 2, rots), mate)
    halo_and_template(
        length_y, across, rim, voxels, raw_ref, block_ref, lk_ref, tz_ref, khat_ref, ext_ref,
        grid_ref, rim_send, rim_recv, peers,
    )

    def forward(step, carry):
        pairs = []
        for i in range(4):
            v = ext_ref[4 * step + i]
            pairs.append(jnp.concatenate([v, v * v], axis=1))
        for which, (re, im) in enumerate(planes(pairs, ly_ref[...], tz_ref[...], length_y)):
            fields[which % 2, 4 * step + which // 2, :, :LANES] = re
            fields[which % 2, 4 * step + which // 2, :, LANES:] = im
        return carry

    lax.fori_loop(0, size_in // 4, forward, 0)
    rows[:, length_y:, :] = jnp.zeros((rows.shape[0], padded - length_y, 2 * LANES), jnp.float32)
    fetch.wait()

    def block(r, carry):
        at = pl.ds(pl.multiple_of(r * 8, 8), 8)

        def first(read, slot):
            for n2 in range(inner):
                values = [read(inner * n1 + n2) for n1 in range(outer)]
                for k1, value in enumerate(small_dft(values, -1)):
                    re, im = turn(value, -n2 * k1, length_x)
                    stage[slot, k1 * inner + n2, :, :LANES] = re
                    stage[slot, k1 * inner + n2, :, LANES:] = im

        def field_reader(which):
            def read(n):
                if n >= size_in:
                    return None
                return (fields[which, n, at, :LANES], fields[which, n, at, LANES:])

            return read

        def kernel_reader(n):
            if n not in places:
                return None
            q = places.index(n)
            return (khat_ref[q, at, :LANES], khat_ref[q, at, LANES:])

        first(field_reader(0), 0)
        first(field_reader(1), 1)
        first(kernel_reader, 2)

        def second(slot, k1):
            values = [
                (stage[slot, k1 * inner + n2, :, :LANES], stage[slot, k1 * inner + n2, :, LANES:])
                for n2 in range(inner)
            ]
            return small_dft(values, -1)

        def times(a, b):
            return (a[0] * b[0] + a[1] * b[1], a[1] * b[0] - a[0] * b[1])

        for k1 in range(outer):
            volume = second(0, k1)
            template = second(2, k1)
            mask = [
                (mhat[k1 + outer * k2, at, :LANES], mhat[k1 + outer * k2, at, LANES:])
                for k2 in range(inner)
            ]
            square = second(1, k1)
            products = (
                [times(a, b) for a, b in zip(volume, template)],
                [times(a, b) for a, b in zip(volume, mask)],
                [times(a, b) for a, b in zip(square, mask)],
            )
            for slot, product in enumerate(products):
                for n2, value in enumerate(small_dft(product, 1)):
                    re, im = turn(value, n2 * k1, length_x)
                    mixed[slot, k1 * inner + n2, :, :LANES] = re
                    mixed[slot, k1 * inner + n2, :, LANES:] = im

        for n2 in range(inner):
            def load(slot):
                return [
                    (mixed[slot, k1 * inner + n2, :, :LANES], mixed[slot, k1 * inner + n2, :, LANES:])
                    for k1 in range(outer)
                ]

            sums = small_dft(load(0), 1)
            for n1 in range(size_x // inner):
                rows[inner * n1 + n2, at, :LANES] = sums[n1][0]
                rows[inner * n1 + n2, at, LANES:] = sums[n1][1]
            for slot in (1, 2):
                re_sum = None
                for k1, (re, im) in enumerate(load(slot)):
                    c, s = phase_ref[me, 2 * k1], phase_ref[me, 2 * k1 + 1]
                    re_part, im_part = re * c - im * s, re * s + im * c
                    if re_sum is None:
                        re_sum, im_sum = re_part, im_part
                    else:
                        re_sum, im_sum = re_sum + re_part, im_sum + im_part
                target = size_x + (slot - 1) * inner + n2
                rows[target, at, :LANES] = re_sum
                rows[target, at, LANES:] = im_sum
        return carry

    lax.fori_loop(0, length_y // 8, block, 0)

    def inverse(part):
        flat = []
        for i in range(inner):
            o = dot(iy_ref[...], pieces(rows[part * inner + i], 0))
            c, s = o[:size_y], o[size_y:]
            re = c[:, :LANES] - s[:, LANES:]
            im = c[:, LANES:] + s[:, :LANES]
            flat.append(jnp.concatenate([re, im], axis=1))
        result = dot(pieces(jnp.concatenate(flat, axis=0), 1), iz_ref[...])
        return result.reshape(inner, size_y, LANES)

    copies = []
    for slot, peer in enumerate(peers):
        local[slot] = inverse(peer)
        copy = pltpu.make_async_remote_copy(
            src_ref=local.at[slot],
            dst_ref=others.at[slot],
            send_sem=send_sem.at[slot],
            recv_sem=recv_sem.at[slot],
            device_id={"rot": peer},
            device_id_type=pl.DeviceIdType.MESH,
        )
        copy.start()
        copies.append(copy)
    mean = inverse(rots) / voxels
    square = inverse(rots + 1) / voxels
    std = jnp.sqrt(jnp.maximum(square - mean * mean, VAR_FLOOR))
    scale = SHARPNESS / (math.sqrt(voxels) * std)
    scores = [inverse(me) * scale]
    for copy in copies:
        copy.wait()
    for slot in range(len(peers)):
        scores.append(others[slot] * scale)
    largest = functools.reduce(jnp.maximum, scores)
    largest_ref[...] = largest
    total_ref[...] = functools.reduce(jnp.add, [jnp.exp(score - largest) for score in scores])


def row_halo(block, across):
    tiles = lax.axis_size("tile")
    up = [(t - across, t) for t in range(across, tiles)]
    down = [(t, s) for s, t in up]
    lower = lax.ppermute(block[block.shape[0] - HALF :], "tile", up)
    upper = lax.ppermute(block[:HALF], "tile", down)
    return jnp.concatenate([lower, block, upper], axis=0)


def shards(volume, templates, rot_ids):
    tile_count = lax.axis_size("tile")
    rots = lax.axis_size("rot")
    across = min(tile_count, 8)
    down = tile_count // across
    block = volume[0]
    size_x, size_y, size_z = block.shape
    inner = size_x // rots
    if down > 1:
        block = row_halo(block, across)
        length_x = size_x + TMPL
        places = tuple(range(TMPL))
    else:
        length_x = -(-(size_x + HALF) // (2 * inner)) * 2 * inner
        places = tuple((q - HALF) % length_x for q in range(TMPL))
    outer = length_x // inner
    size_in = block.shape[0]
    length_y = size_y + TMPL
    padded = -(-length_y // 16) * 16
    length_z = size_z + HALF
    freqs = length_z // 2 + 1

    mask = sphere()
    voxels = float(mask.sum())
    rim = -(-HALF // 8) * 8
    reach = size_y + 2 * rim
    tz = jnp.asarray(z_forward(length_z, LANES, freqs))
    kernel_rows = 48
    grid = templates[rot_ids[0]].reshape(TMPL, TMPL, TMPL)
    vmem = pl.BlockSpec(memory_space=pltpu.VMEM)
    mhat = jnp.asarray(mask_spectrum(places, length_x, length_y, length_z, freqs))
    turns = angles(outer, np.arange(rots), np.arange(outer))
    phase = jnp.asarray(np.stack([np.cos(turns), np.sin(turns)], axis=2).reshape(rots, 2 * outer).astype(np.float32))
    dims = (size_in, length_y, padded, size_x, size_y, inner, outer, across, rim)
    largest, total = pl.pallas_call(
        functools.partial(main_kernel, dims, places, voxels),
        out_shape=(
            jax.ShapeDtypeStruct((inner, size_y, size_z), jnp.float32),
            jax.ShapeDtypeStruct((inner, size_y, size_z), jnp.float32),
        ),
        in_specs=[
            vmem, vmem, pl.BlockSpec(memory_space=pl.ANY), pl.BlockSpec(memory_space=pltpu.SMEM),
            vmem, vmem, vmem, vmem, vmem,
        ],
        out_specs=(vmem, vmem),
        scratch_shapes=[
            pltpu.VMEM((TMPL, kernel_rows, LANES), jnp.float32),
            pltpu.VMEM((size_in, reach, size_z), jnp.float32),
            pltpu.VMEM((2, size_in, length_y, 2 * LANES), jnp.float32),
            pltpu.VMEM((TMPL, length_y, 2 * LANES), jnp.float32),
            pltpu.VMEM((length_x, length_y, 2 * LANES), jnp.float32),
            pltpu.VMEM((3, length_x, 8, 2 * LANES), jnp.float32),
            pltpu.VMEM((3, length_x, 8, 2 * LANES), jnp.float32),
            pltpu.VMEM((size_x + 2 * inner, padded, 2 * LANES), jnp.float32),
            pltpu.VMEM((rots - 1, inner, size_y, size_z), jnp.float32),
            pltpu.VMEM((rots - 1, inner, size_y, size_z), jnp.float32),
            pltpu.SemaphoreType.DMA,
            pltpu.SemaphoreType.DMA((4,)),
            pltpu.SemaphoreType.DMA((4,)),
            pltpu.SemaphoreType.DMA((rots - 1,)),
            pltpu.SemaphoreType.DMA((rots - 1,)),
        ],
        compiler_params=pltpu.CompilerParams(vmem_limit_bytes=VMEM, collective_id=0, has_side_effects=True),
        name="correlate",
    )(
        grid, block, mhat, phase,
        jnp.asarray(y_forward(length_y, kernel_rows, 0)),
        jnp.asarray(y_forward(length_y, reach, rim - HALF)), tz,
        jnp.asarray(y_inverse(length_y, padded, size_y)),
        jnp.asarray(z_inverse(length_z, size_z, freqs, length_x)),
    )
    return (largest + jnp.log(total))[None]


def solution(mesh):
    return jax.shard_map(
        shards,
        mesh=mesh,
        in_specs=(P("tile", None, None, None), P(), P("rot")),
        out_specs=P("tile", "rot", None, None),
        check_vma=False,
    )
```
